32 devices in a mesh: hist: 16 (over z, y, x), batch: 2 (over core).
Axes of the slice: x: 2, y: 2, z: 4, core: 2. Of those that a mesh axis runs over, the one named last changes fastest.
Arguments:
- targets: bfloat16 [2, 4096, 512], P('batch', 'hist'), may hold values from -6 to 6
- w_query: bfloat16 [512, 1024], replicated, may hold values from -0.25 to 0.25
- keys: bfloat16 [2, 2048, 1024], P('batch', 'hist'), may hold values from -64 to 64
- values: bfloat16 [2, 2048, 1024], P('batch', 'hist'), may hold values from -12 to 12
- blocks: int32 [2, 8, 16], P('batch'), may hold values from 0 to 31, as said below
- lengths: int32 [2], P('batch'), may hold values from 1921 to 2048, as said below
- d_attended: bfloat16 [2, 4096, 1024], P('batch', 'hist'), may hold values from -6 to 6
Outputs:
- attended: bfloat16 [2, 4096, 1024], P('batch', 'hist')
- d_targets: bfloat16 [2, 4096, 512], P('batch', 'hist')
- d_query_weight: float32 [512, 1024], P(('hist', 'batch'))
The draws below stay inside these ranges and needn't reach their ends.
Inputs may be any that keep to these rules, and one draw needn't show every extreme that they name: `lengths`: one user in every draw has the whole history of 2048 slots. Each list names 16 distinct blocks, all live. Its first entry is the block holding the user's last behavior; the others lie in the ranges of different hist indices (2 blocks a range), none in the range of that last block, so a range holds at most one block of a list.
All inputs are finite; a program needn't handle non-finite values.
Results may differ from the reference program's by a relative error of at most 0.01.
The reference program's roundings to bfloat16 on the way count: a program that leaves them out, or rounds other values in their place, can miss the bound.
Values may be sent and summed in bfloat16 or wider, within the bound.
No kernel may reach another device: no remote copies, remote signals or barrier semaphores. Data moves between devices by JAX's collectives and lax.ppermute only.
A program may use at most 64 MiB of HBM per device.

```python
import jax
import jax.numpy as jnp
from jax import lax

HEADS = 8
DH = 128
E = 512
BLK = 64
TOPK = 16
BLK_DEV = 2
USERS = 2
NBLK = 32
HIST_LEN = 2048
CANDS = 4096
HD = 1024
N_HIST = 16


def history_plan(key):
    key_len, key_full, key_perm, key_off = jax.random.split(key, 4)
    shortest = (TOPK - 1) * BLK * BLK_DEV + 1
    lens = jax.random.randint(key_len, (USERS,), shortest, HIST_LEN + 1)
    full = jax.random.randint(key_full, (), 0, USERS)
    lens = jnp.where(jnp.arange(USERS) == full, HIST_LEN, lens).astype(jnp.int32)
    span = BLK * BLK_DEV
    live_blocks = (lens + BLK - 1) // BLK
    live_owners = (lens + span - 1) // span
    last_block = live_blocks - 1
    last_owner = last_block // BLK_DEV
    owner_ids = jnp.arange(N_HIST, dtype=jnp.int32)
    barred = (owner_ids[None, :] >= live_owners[:, None]) | (owner_ids[None, :] == last_owner[:, None])
    noise = jax.random.randint(key_perm, (USERS, HEADS, N_HIST), 0, 1 << 20)
    scores = noise * N_HIST + owner_ids[None, None, :] + barred[:, None, :].astype(jnp.int32) * ((1 << 20) * N_HIST)
    owners = jnp.argsort(scores, axis=-1)[..., :TOPK - 1].astype(jnp.int32)
    owned_count = jnp.minimum(BLK_DEV, live_blocks[:, None, None] - owners * BLK_DEV)
    offset = jax.random.randint(key_off, (USERS, HEADS, TOPK - 1), 0, 1 << 20) % owned_count
    others = owners * BLK_DEV + offset
    first = jnp.broadcast_to(last_block[:, None, None], (USERS, HEADS, 1))
    chosen = jnp.concatenate([first, others], axis=-1).astype(jnp.int32)
    return (lens, chosen)


def draw_lengths(key, part):
    lens, chosen = history_plan(key)
    return lens


def draw_blocks(key, part):
    lens, chosen = history_plan(key)
    return chosen


def draw_keys(key, part):
    key = jax.random.fold_in(key, 11)
    key_base = jax.random.fold_in(key, 0)
    shape = (USERS, HIST_LEN, HEADS, DH)
    base = jnp.clip(jax.random.normal(key_base, shape, jnp.float32), -6.0, 6.0)
    return base.reshape(USERS, HIST_LEN, HEADS * DH).astype(jnp.bfloat16)


def with_spikes(array, key, source, target, blocks, factor):
    owner, partner = [(jnp.arange(array.shape[axis_at]) // (array.shape[axis_at] // blocks)).reshape([-1 if axis == axis_at else 1 for axis in range(array.ndim)]) for axis_at in (source, target)]
    chosen = jax.random.permutation(key, blocks)[partner]
    strong = (owner == chosen) | (owner == (partner + blocks // 2) % blocks)
    return jnp.where(strong, factor * array, array)


def level_of(own_key, shape, cuts, smallest, top_value):
    factor_of, own = 1.0, jax.random.fold_in(own_key, 6)
    for axis_at, blocks in cuts:
        steps = jnp.exp(jax.random.uniform(jax.random.fold_in(own, axis_at), (blocks,), jnp.float32, smallest / len(cuts), top_value / len(cuts)))
        factor_of = factor_of * jnp.repeat(steps, shape[axis_at] // blocks).reshape([-1 if axis == axis_at else 1 for axis in range(len(shape))])
    return factor_of


def normal_values(own_key, extent, deviation, limit, cuts=(), kind=jnp.bfloat16):
    drawn = deviation * jax.random.normal(own_key, extent, jnp.float32)
    if cuts:
        drawn = drawn * level_of(own_key, extent, cuts, -0.22, 0.18)
    return jnp.clip(drawn, -limit, limit).astype(kind)


def heavy_noise(own_key, shape, width, limit, cuts, heavy, held_as=jnp.bfloat16):
    values = width * jax.random.normal(own_key, shape, jnp.float32)
    if cuts:
        values = values * level_of(own_key, shape, cuts, -0.22, 0.18)
    return jnp.clip(with_spikes(values, jax.random.fold_in(own_key, 3), *heavy), -limit, limit).astype(held_as)


def setup_inputs(seed: int = 0) -> dict:
    arg_keys = jax.random.split(jax.random.key(seed), 8)
    return {
        "targets": heavy_noise(arg_keys[0], (USERS, CANDS, E), 1.0, 6.0, ((0, 2), (1, 16)), (1, 2, 16, 2.0)),
        "w_query": normal_values(arg_keys[1], (E, HD), E ** -0.5, 0.25),
        "keys": draw_keys(jax.random.fold_in(arg_keys[7], 71), 0),
        "values": normal_values(arg_keys[3], (USERS, HIST_LEN, HD), 2.0, 12.0, ((0, 2), (1, 16))),
        "blocks": draw_blocks(jax.random.fold_in(arg_keys[7], 71), 0),
        "lengths": draw_lengths(jax.random.fold_in(arg_keys[7], 71), 0),
        "d_attended": normal_values(arg_keys[6], (USERS, CANDS, HD), 1.0, 6.0, ((0, 2), (1, 16))),
    }


def summarize(rows, live, block):
    count = rows.shape[0] // block
    kept = jnp.where(live[:, None], rows.astype(jnp.float32), 0.0)
    total = jnp.sum(kept.reshape(count, block, rows.shape[1]), axis=1)
    return (total * block ** -0.5).astype(jnp.bfloat16)


def attend(query, key_part, value_part, valid, grad, scale):
    scores = jnp.dot(query, key_part.T, preferred_element_type=jnp.float32) * scale
    masked = jnp.where(valid[None, :], scores, -jnp.inf)
    top = jnp.max(masked, axis=1, keepdims=True)
    expo = jnp.where(valid[None, :], jnp.exp(scores - top), 0.0)
    probs = expo / jnp.sum(expo, axis=1, keepdims=True)
    result = jnp.dot(probs.astype(jnp.bfloat16), value_part, preferred_element_type=jnp.float32)
    d_probs = jnp.dot(grad, value_part.T, preferred_element_type=jnp.float32)
    d_scores = probs * (d_probs - jnp.sum(probs * d_probs, axis=1, keepdims=True))
    d_query = jnp.dot(d_scores.astype(jnp.bfloat16), key_part, preferred_element_type=jnp.float32) * scale
    return result, d_query


def reference(targets, w_query, keys, values, blocks, lengths, d_attended):
    scale = DH ** -0.5

    def one_user(packed):
        target_rows, key_rows, value_rows, chosen, length, grad = packed
        query = jnp.dot(target_rows, w_query, preferred_element_type=jnp.float32).astype(jnp.bfloat16)
        live = jnp.arange(HIST_LEN, dtype=jnp.int32) < length
        summary_keys = summarize(key_rows, live, BLK)
        summary_values = summarize(value_rows, live, BLK)
        summary_live = jnp.arange(NBLK, dtype=jnp.int32) * BLK < length

        def one_head(head):
            start = (head * DH).astype(jnp.int32)
            q_head = lax.dynamic_slice_in_dim(query, start, DH, 1)
            g_head = lax.dynamic_slice_in_dim(grad, start, DH, 1)
            coarse, coarse_dq = attend(q_head, lax.dynamic_slice_in_dim(summary_keys, start, DH, 1),
                                       lax.dynamic_slice_in_dim(summary_values, start, DH, 1),
                                       summary_live, g_head, scale)
            picked = chosen[head]
            tokens = (picked[:, None] * BLK + jnp.arange(BLK, dtype=jnp.int32)[None, :]).reshape(TOPK * BLK)
            tokens = tokens.astype(jnp.int32)
            near_keys = jnp.take(lax.dynamic_slice_in_dim(key_rows, start, DH, 1), tokens, axis=0)
            near_values = jnp.take(lax.dynamic_slice_in_dim(value_rows, start, DH, 1), tokens, axis=0)
            near, near_dq = attend(q_head, near_keys, near_values, tokens < length, g_head, scale)
            return coarse + near, coarse_dq + near_dq

        outs, grads = lax.map(one_head, jnp.arange(HEADS, dtype=jnp.int32))
        attended = jnp.transpose(outs, (1, 0, 2)).reshape(CANDS, HD).astype(jnp.bfloat16)
        d_query = jnp.transpose(grads, (1, 0, 2)).reshape(CANDS, HD).astype(jnp.bfloat16)
        d_target = jnp.dot(d_query, w_query.T, preferred_element_type=jnp.float32).astype(jnp.bfloat16)
        term = jnp.dot(target_rows.T, d_query, preferred_element_type=jnp.float32)
        return attended, d_target, term

    attended, d_targets, terms = lax.map(one_user, (targets, keys, values, blocks, lengths, d_attended))
    return attended, d_targets, jnp.sum(terms, axis=0)
```

```python
import functools

import jax
import jax.numpy as jnp
from jax import lax
from jax.experimental import pallas as pl
from jax.experimental.pallas import tpu as pltpu
from jax.sharding import PartitionSpec as P

BLK = 64
LANES = 128
QUAD = 4
DEAD = -1e30
VMEM_LIMIT = 60 * 1024 * 1024
F32 = jnp.float32
BF16 = jnp.bfloat16


def swap(array, axis, mask):
    size = lax.axis_size(axis)
    return lax.ppermute(array, axis, [(i, i ^ mask) for i in range(size)])


def select_kernel(cuts, blocks_ref, lengths_ref, keys_ref, values_ref, *outs):
    heads, topk = blocks_ref.shape[1:]
    rows, width = keys_ref.shape[1:]
    head_dim = width // heads
    blk_dev = rows // BLK
    rank = lax.axis_index("hist")
    length = lengths_ref[0]
    for out, (first, last) in zip(outs, cuts):
        for head in range(first, last):
            local = jnp.int32(0)
            for entry in range(topk):
                block = blocks_ref[0, head, entry] - rank * blk_dev
                local = jnp.where((block >= 0) & (block < blk_dev), block, local)
            low = pl.multiple_of(local * BLK, BLK)
            at = (head - first) * BLK
            columns = slice(head * head_dim, (head + 1) * head_dim)
            out[at : at + BLK, :head_dim] = keys_ref[0, pl.ds(low, BLK), columns]
            out[at : at + BLK, head_dim:] = values_ref[0, pl.ds(low, BLK), columns]
    sums = []
    for source in (keys_ref, values_ref):
        totals = []
        for block in range(blk_dev):
            part = source[0, block * BLK : (block + 1) * BLK, :].astype(F32)
            spot = lax.broadcasted_iota(jnp.int32, part.shape, 0) + (
                rank * rows + block * BLK
            )
            part = jnp.where(spot < length, part, 0.0)
            totals.append(jnp.sum(part, axis=0, keepdims=True) * BLK ** (-0.5))
        sums.append(
            jnp.concatenate(
                [
                    totals[block][:, head * head_dim : (head + 1) * head_dim]
                    for head in range(heads)
                    for block in range(blk_dev)
                ],
                axis=0,
            )
        )
    at = (cuts[0][1] - cuts[0][0]) * BLK
    count = heads * blk_dev
    outs[0][at : at + count, :head_dim] = sums[0].astype(BF16)
    outs[0][at : at + count, head_dim:] = sums[1].astype(BF16)


def attend_kernel(pieces, fine_width, scale, *refs):
    query_ref, grad_ref, bias_ref, summary_ref = refs[:4]
    piece_refs = refs[4 : 4 + pieces]
    out_ref, dq_ref = refs[-2:]
    head_dim = query_ref.shape[1]
    keys = jnp.concatenate(
        [r[:, :, :head_dim].reshape(-1, head_dim) for r in piece_refs]
        + [summary_ref[0, :, :head_dim]],
        axis=0,
    )
    values = jnp.concatenate(
        [r[:, :, head_dim:].reshape(-1, head_dim) for r in piece_refs]
        + [summary_ref[0, :, head_dim:]],
        axis=0,
    )
    bias = bias_ref[0]
    cols = (slice(0, fine_width), slice(fine_width, keys.shape[0]))
    step = min(128, query_ref.shape[0])
    contract = (((1,), (1,)), ((), ()))
    for low in range(0, query_ref.shape[0], step):
        rows = slice(low, low + step)
        query = query_ref[rows, :]
        grad = grad_ref[0, rows, :]
        scores = lax.dot_general(query, keys, contract, preferred_element_type=F32) * scale + bias
        d_probs = lax.dot_general(grad, values, contract, preferred_element_type=F32)
        probs_parts = []
        d_parts = []
        for part in cols:
            score = scores[:, part]
            expo = jnp.exp(score - jnp.max(score, axis=1, keepdims=True))
            probs = expo * (1.0 / jnp.sum(expo, axis=1, keepdims=True))
            d_prob = d_probs[:, part]
            delta = jnp.sum(probs * d_prob, axis=1, keepdims=True)
            probs_parts.append(probs.astype(BF16))
            d_parts.append((probs * (d_prob - delta)).astype(BF16))
        out = jnp.dot(jnp.concatenate(probs_parts, axis=1), values, preferred_element_type=F32)
        d_query = jnp.dot(jnp.concatenate(d_parts, axis=1), keys, preferred_element_type=F32)
        out_ref[0, rows, :] = out.astype(BF16)
        dq_ref[0, rows, :] = (d_query * scale).astype(BF16)


def attend(first, count, query, grad, bias, summary, pieces, earlier):
    rows, width = query.shape
    heads = bias.shape[0]
    head_dim = width // heads
    fine_width = sum(p.shape[0] for p in pieces) * BLK
    whole = pl.BlockSpec((1, rows, head_dim), lambda i: (0, 0, first + i))
    in_specs = [
        pl.BlockSpec((rows, head_dim), lambda i: (0, first + i)),
        whole,
        pl.BlockSpec((1,) + bias.shape[1:], lambda i: (first + i, 0, 0)),
        pl.BlockSpec((1,) + summary.shape[1:], lambda i: (first + i, 0, 0)),
    ]
    in_specs += [
        pl.BlockSpec((p.shape[0], BLK, 2 * head_dim), lambda i: (0, i, 0)) for p in pieces
    ]
    args = [query, grad, bias, summary, *pieces]
    aliases = {}
    if earlier is not None:
        aliases = {len(args): 0, len(args) + 1: 1}
        args += list(earlier)
        in_specs += [pl.BlockSpec(memory_space=pl.ANY)] * 2
    shape = jax.ShapeDtypeStruct((1, rows, width), BF16)
    columns = bias.shape[-1]
    return pl.pallas_call(
        functools.partial(attend_kernel, len(pieces), fine_width, head_dim ** (-0.5)),
        grid=(count,),
        in_specs=in_specs,
        out_specs=(whole, whole),
        out_shape=(shape, shape),
        input_output_aliases=aliases,
        compiler_params=pltpu.CompilerParams(vmem_limit_bytes=VMEM_LIMIT),
        cost_estimate=pl.CostEstimate(
            flops=8 * count * rows * columns * head_dim,
            bytes_accessed=count * (columns * 512 + rows * head_dim * 8),
            transcendentals=count * rows * columns,
        ),
        name="attend",
    )(*args)


def gather(part, sync):
    size = lax.axis_size("hist")
    if sync is not None:
        part, _ = lax.optimization_barrier((part, sync))
    column = jnp.stack(
        [part] + [swap(part, "hist", QUAD * k) for k in range(1, size // QUAD)]
    )
    half = column.shape[0] // 2
    across = swap(column, "hist", 1)
    along = swap(column, "hist", 2)
    far = (swap(across[:half], "hist", 2), swap(along[half:], "hist", 1))
    return (column, across, along) + far


def spread(total, axis, masks, weight):
    result = total[0]
    for index in range(1, masks):
        result = result + swap(total[index].astype(BF16), axis, weight * index).astype(F32)
    return result


def shards(targets, w_query, keys, values, blocks, lengths, d_attended):
    heads = blocks.shape[1]
    local_rows, width = keys.shape[1:]
    head_dim = width // heads
    blk_dev = local_rows // BLK
    n_hist = lax.axis_size("hist")
    n_batch = lax.axis_size("batch")
    rank = lax.axis_index("hist")
    lane = lax.axis_index("batch")
    rows = targets.shape[1]
    depth = targets.shape[2]

    cut = heads // 2
    cuts = ((0, cut), (cut, heads))
    sizes = [(last - first) * BLK for first, last in cuts]
    sizes[0] += heads * blk_dev
    picked = pl.pallas_call(
        functools.partial(select_kernel, cuts),
        in_specs=[
            pl.BlockSpec(memory_space=pltpu.SMEM),
            pl.BlockSpec(memory_space=pltpu.SMEM),
            pl.BlockSpec(memory_space=pltpu.VMEM),
            pl.BlockSpec(memory_space=pltpu.VMEM),
        ],
        out_specs=[pl.BlockSpec(memory_space=pltpu.VMEM)] * len(cuts),
        out_shape=[jax.ShapeDtypeStruct((size, 2 * head_dim), BF16) for size in sizes],
        name="select",
    )(blocks, lengths, keys, values)

    near = gather(picked[0], None)
    late = gather(picked[1], near[0])

    query = jnp.dot(targets[0], w_query, preferred_element_type=F32).astype(BF16)

    masks = jnp.asarray([q + QUAD * k for q in range(QUAD) for k in range(n_hist // QUAD)], jnp.int32)
    source = rank ^ masks
    owner = blocks[0] // blk_dev
    listed = jnp.max(
        jnp.where(owner[:, :, None] == source[None, None, :], blocks[0][:, :, None], -1), axis=1
    )
    spots = jnp.arange(BLK, dtype=jnp.int32)
    live = (listed[:, :, None] >= 0) & (listed[:, :, None] * BLK + spots < lengths[0])
    fine_bias = jnp.where(live, 0.0, DEAD).astype(F32).reshape(heads, -1)
    names = (source[:, None] * blk_dev + jnp.arange(blk_dev, dtype=jnp.int32)).reshape(-1)
    padded = -(-names.shape[0] // LANES) * LANES
    extra = padded - names.shape[0]
    coarse_bias = jnp.where(names * BLK < lengths[0], 0.0, DEAD).astype(F32)
    coarse_bias = jnp.pad(coarse_bias, (0, extra), constant_values=DEAD)
    bias = jnp.concatenate(
        [fine_bias, jnp.broadcast_to(coarse_bias[None], (heads, padded))], axis=1
    )[:, None, :]
    start = sizes[0] - heads * blk_dev
    summary = jnp.concatenate([p[:, start:] for p in near], axis=0)
    summary = summary.reshape(n_hist, heads, blk_dev, 2 * head_dim).transpose(1, 0, 2, 3)
    summary = summary.reshape(heads, n_hist * blk_dev, 2 * head_dim)
    summary = jnp.pad(summary, ((0, 0), (0, extra), (0, 0)))

    places = (
        (rank ^ masks)[None, :] * n_batch + (lane ^ jnp.arange(n_batch, dtype=jnp.int32))[:, None]
    ).reshape(-1)
    share = depth // (n_hist * n_batch)
    chosen = (places[:, None] * share + jnp.arange(share, dtype=jnp.int32)).reshape(-1)
    shuffle = (jnp.arange(depth, dtype=jnp.int32)[:, None] == chosen[None, :]).astype(BF16)
    ordered = jnp.dot(targets[0], shuffle, preferred_element_type=F32).astype(BF16)

    done = attend(0, cut, query, d_attended, bias, summary, near, None)
    attended, d_query = attend(cut, heads - cut, query, d_attended, bias, summary, late, done)

    total = lax.dot_general(
        ordered, d_query[0], (((0,), (0,)), ((), ())), preferred_element_type=F32
    )
    total = total.reshape(n_batch, QUAD, n_hist // QUAD, share, width)
    total = spread(total, "batch", n_batch, 1)
    total = spread(total, "hist", QUAD, 1)
    d_query_weight = spread(total, "hist", n_hist // QUAD, QUAD)
    d_targets = lax.dot_general(
        d_query[0], w_query, (((1,), (1,)), ((), ())), preferred_element_type=F32
    ).astype(BF16)
    return (attended, d_targets[None], d_query_weight)


def solution(mesh):
    in_specs = (
        P("batch", "hist", None),
        P(),
        P("batch", "hist", None),
        P("batch", "hist", None),
        P("batch", None, None),
        P("batch"),
        P("batch", "hist", None),
    )
    out_specs = (P("batch", "hist", None), P("batch", "hist", None), P(("hist", "batch"), None))
    return jax.shard_map(shards, mesh=mesh, in_specs=in_specs, out_specs=out_specs, check_vma=False)
```

```python
import functools

import jax
import jax.numpy as jnp
from jax import lax
from jax.experimental import pallas as pl
from jax.experimental.pallas import tpu as pltpu
from jax.sharding import PartitionSpec as P

BLK = 64
LANES = 128
TILE = 16
QUAD = 4
PAIR = 2
DEAD = -1e30
VMEM_LIMIT = 60 * 1024 * 1024
CUT = 2
STEP = 256
F32 = jnp.float32
BF16 = jnp.bfloat16


def swap(array, axis, mask):
    size = lax.axis_size(axis)
    return lax.ppermute(array, axis, [(i, i ^ mask) for i in range(size)])


def after(array, other):
    return lax.optimization_barrier((array, other))[0]


def select_kernel(cut, blocks_ref, lengths_ref, keys_ref, values_ref, *outs):
    heads, topk = blocks_ref.shape[1:]
    rows, width = keys_ref.shape[1:]
    half = heads // PAIR
    head_dim = width // heads
    blk_dev = rows // BLK
    rank = lax.axis_index("hist")
    side = (rank // QUAD) % PAIR
    length = lengths_ref[0]
    count = half * blk_dev
    room = -(-count // TILE) * TILE
    for out, first in zip(outs, (side * half, (1 - side) * half)):
        for index in range(half):
            head = first + index
            local = jnp.int32(0)
            for entry in range(topk):
                block = blocks_ref[0, head, entry] - rank * blk_dev
                local = jnp.where((block >= 0) & (block < blk_dev), block, local)
            low = pl.multiple_of(local * BLK, BLK)
            at = index * BLK + (room if index >= cut else 0)
            columns = pl.ds(pl.multiple_of(head * head_dim, head_dim), head_dim)
            out[at : at + BLK, :head_dim] = keys_ref[0, pl.ds(low, BLK), columns]
            out[at : at + BLK, head_dim:] = values_ref[0, pl.ds(low, BLK), columns]
        span = pl.ds(pl.multiple_of(first * head_dim, head_dim), half * head_dim)
        for source, low in ((keys_ref, 0), (values_ref, head_dim)):
            totals = []
            for block in range(blk_dev):
                part = source[0, block * BLK : (block + 1) * BLK, span].astype(F32)
                spot = lax.broadcasted_iota(jnp.int32, part.shape, 0) + (rank * rows + block * BLK)
                part = jnp.where(spot < length, part, 0.0)
                totals.append(jnp.sum(part, axis=0, keepdims=True) * BLK ** (-0.5))
            lines = [
                totals[block][:, index * head_dim : (index + 1) * head_dim]
                for index in range(half)
                for block in range(blk_dev)
            ]
            lines.append(jnp.zeros((room - count, head_dim), F32))
            summary = jnp.concatenate(lines, axis=0).astype(BF16)
            out[cut * BLK : cut * BLK + room, low : low + head_dim] = summary


def attend_kernel(pieces, fine_width, scale, *refs):
    query_ref, grad_ref, bias_ref, ordered_ref = refs[:4]
    piece_refs = refs[4 : 4 + 2 * pieces]
    out_ref, dq_ref, away_ref, keep_ref, send_ref = refs[-5:]
    head_dim = query_ref.shape[1]
    keys = jnp.concatenate(
        [r[:, :, :head_dim].reshape(-1, head_dim) for r in piece_refs], axis=0
    )
    values = jnp.concatenate(
        [r[:, :, head_dim:].reshape(-1, head_dim) for r in piece_refs], axis=0
    )
    bias = bias_ref[0]
    cols = (slice(0, fine_width), slice(fine_width, keys.shape[0]))
    rows = out_ref.shape[0]
    step = min(STEP, rows)
    contract = (((1,), (1,)), ((), ()))
    d_queries = []
    places = ((out_ref, dq_ref, 0), (away_ref.at[0], away_ref.at[1], rows))
    for out_part, dq_part, base in places:
        for low in range(0, rows, step):
            query = query_ref[base + low : base + low + step, :]
            grad = grad_ref[base + low : base + low + step, :]
            scores = lax.dot_general(query, keys, contract, preferred_element_type=F32) * scale + bias
            d_probs = lax.dot_general(grad, values, contract, preferred_element_type=F32)
            probs_parts = []
            d_parts = []
            for part in cols:
                score = scores[:, part]
                expo = jnp.exp(score - jnp.max(score, axis=1, keepdims=True))
                probs = expo * (1.0 / jnp.sum(expo, axis=1, keepdims=True))
                d_prob = d_probs[:, part]
                delta = jnp.sum(probs * d_prob, axis=1, keepdims=True)
                probs_parts.append(probs.astype(BF16))
                d_parts.append((probs * (d_prob - delta)).astype(BF16))
            out = jnp.dot(jnp.concatenate(probs_parts, axis=1), values, preferred_element_type=F32)
            d_query = jnp.dot(jnp.concatenate(d_parts, axis=1), keys, preferred_element_type=F32)
            d_query = (d_query * scale).astype(BF16)
            out_part[low : low + step, :] = out.astype(BF16)
            dq_part[low : low + step, :] = d_query
            d_queries.append(d_query)
    weight = jnp.dot(
        ordered_ref[...], jnp.concatenate(d_queries, axis=0), preferred_element_type=F32
    )
    kept = keep_ref.shape[0]
    keep_ref[...] = weight[:kept]
    send_ref[...] = weight[kept:].astype(BF16)


def attend(first, count, query, grad, bias, ordered, summaries, pieces, share, earlier):
    rows, width = query.shape
    half = bias.shape[0]
    head_dim = width // half
    fine_width = sum(p.shape[0] for p in pieces) * BLK
    room = (bias.shape[-1] - fine_width) // sum(p.shape[0] for p in pieces)
    depth = ordered.shape[0]
    kept = depth // share
    in_specs = [
        pl.BlockSpec((rows, head_dim), lambda i: (0, first + i)),
        pl.BlockSpec((rows, head_dim), lambda i: (0, first + i)),
        pl.BlockSpec((1,) + bias.shape[1:], lambda i: (first + i, 0, 0)),
        pl.BlockSpec(ordered.shape, lambda i: (0, 0)),
    ]
    in_specs += [
        pl.BlockSpec((p.shape[0], BLK, 2 * head_dim), lambda i: (0, i, 0)) for p in pieces
    ]
    in_specs += [
        pl.BlockSpec((p.shape[0], room, 2 * head_dim), lambda i: (0, CUT * BLK // room, 0))
        for p in summaries
    ]
    args = [query, grad, bias, ordered, *pieces, *summaries]
    aliases = {}
    if earlier is not None:
        aliases = {len(args) + i: 3 + i for i in range(len(earlier))}
        args += list(earlier)
        in_specs += [pl.BlockSpec(memory_space=pl.ANY)] * len(earlier)
    own = jax.ShapeDtypeStruct((rows // PAIR, count * head_dim), BF16)
    own_spec = pl.BlockSpec((rows // PAIR, head_dim), lambda i: (0, i))
    columns = bias.shape[-1]
    return pl.pallas_call(
        functools.partial(attend_kernel, len(pieces), fine_width, head_dim ** (-0.5)),
        grid=(count,),
        in_specs=in_specs,
        out_specs=(
            own_spec,
            own_spec,
            pl.BlockSpec((2, rows // PAIR, head_dim), lambda i: (0, 0, i)),
            pl.BlockSpec((kept, head_dim), lambda i: (0, first + i)),
            pl.BlockSpec((depth - kept, head_dim), lambda i: (0, first + i)),
        ),
        out_shape=(
            own,
            own,
            jax.ShapeDtypeStruct((2,) + own.shape, BF16),
            jax.ShapeDtypeStruct((kept, width), F32),
            jax.ShapeDtypeStruct((depth - kept, width), BF16),
        ),
        input_output_aliases=aliases,
        compiler_params=pltpu.CompilerParams(vmem_limit_bytes=VMEM_LIMIT),
        cost_estimate=pl.CostEstimate(
            flops=8 * count * rows * columns * head_dim,
            bytes_accessed=count * (columns * 512 + rows * head_dim * 8),
            transcendentals=count * rows * columns,
        ),
        name="attend",
    )(*args)


def gather_quad(column):
    return [column] + [swap(column, "hist", mask) for mask in range(1, QUAD)]


def gather_rest(pair):
    count = lax.axis_size("hist") // (QUAD * PAIR)
    return jnp.concatenate(
        [pair] + [swap(pair, "hist", QUAD * PAIR * k) for k in range(1, count)], axis=0
    )


def shards(targets, w_query, keys, values, blocks, lengths, d_attended):
    heads = blocks.shape[1]
    local_rows, width = keys.shape[1:]
    head_dim = width // heads
    blk_dev = local_rows // BLK
    n_hist = lax.axis_size("hist")
    n_batch = lax.axis_size("batch")
    rank = lax.axis_index("hist")
    lane = lax.axis_index("batch")
    rows = targets.shape[1]
    depth = targets.shape[2]
    half = heads // PAIR
    side = (rank // QUAD) % PAIR
    wide = half * head_dim
    count = half * blk_dev
    room = -(-count // TILE) * TILE
    first_rows = CUT * BLK + room

    shape = jax.ShapeDtypeStruct((half * BLK + room, 2 * head_dim), BF16)
    keep, send = pl.pallas_call(
        functools.partial(select_kernel, CUT),
        in_specs=[
            pl.BlockSpec(memory_space=pltpu.SMEM),
            pl.BlockSpec(memory_space=pltpu.SMEM),
            pl.BlockSpec(memory_space=pltpu.VMEM),
            pl.BlockSpec(memory_space=pltpu.VMEM),
        ],
        out_specs=[pl.BlockSpec(memory_space=pltpu.VMEM)] * 2,
        out_shape=[shape] * 2,
        name="select",
    )(blocks, lengths, keys, values)
    came = swap(send, "hist", QUAD)
    pair_near = jnp.stack([keep[:first_rows], came[:first_rows]])
    pair_late = jnp.stack([keep[first_rows:], came[first_rows:]])
    column_near = gather_rest(pair_near)
    column_late = gather_rest(after(pair_late, column_near))
    near = gather_quad(column_near)

    grad = d_attended[0]
    grad_keep = lax.dynamic_slice_in_dim(grad, side * wide, wide, 1)
    grad_send = lax.dynamic_slice_in_dim(grad, (1 - side) * wide, wide, 1)
    mine = jnp.concatenate([targets[0], grad_send], axis=0)
    theirs = swap(after(mine, came), "hist", QUAD)
    both_targets = jnp.concatenate([targets[0], theirs[:rows]], axis=0)
    both_grads = jnp.concatenate([grad_keep, theirs[rows:]], axis=0)
    weights = lax.dynamic_slice_in_dim(w_query, side * wide, wide, 1)
    query = jnp.dot(both_targets, weights, preferred_element_type=F32).astype(BF16)

    masks = jnp.asarray([q + QUAD * k for q in range(QUAD) for k in range(n_hist // QUAD)], jnp.int32)
    source = rank ^ masks
    lists = lax.dynamic_slice_in_dim(after(blocks, column_near)[0], side * half, half, 0)
    listed = jnp.max(
        jnp.where((lists // blk_dev)[:, :, None] == source[None, None, :], lists[:, :, None], -1),
        axis=1,
    )
    spots = jnp.arange(BLK, dtype=jnp.int32)
    live = (listed[:, :, None] >= 0) & (listed[:, :, None] * BLK + spots < lengths[0])
    fine_bias = jnp.where(live, 0.0, DEAD).astype(F32).reshape(half, -1)
    line = jnp.arange(room, dtype=jnp.int32)
    names = source[:, None] * blk_dev + line[None, :] % blk_dev
    own_line = (line // blk_dev)[None, :] == jnp.arange(half, dtype=jnp.int32)[:, None]
    coarse_live = own_line[:, None, :] & (names * BLK < lengths[0])[None]
    coarse_bias = jnp.where(coarse_live, 0.0, DEAD).astype(F32).reshape(half, -1)
    bias = jnp.concatenate([fine_bias, coarse_bias], axis=1)[:, None, :]

    places = (
        (rank ^ masks)[None, :] * n_batch + (lane ^ jnp.arange(n_batch, dtype=jnp.int32))[:, None]
    ).reshape(-1)
    share = depth // (n_hist * n_batch)
    chosen = (places[:, None] * share + jnp.arange(share, dtype=jnp.int32)).reshape(-1)
    shuffle = (chosen[:, None] == jnp.arange(depth, dtype=jnp.int32)[None, :]).astype(BF16)
    ordered = lax.dot_general(
        shuffle, both_targets, (((1,), (1,)), ((), ())), preferred_element_type=F32
    ).astype(BF16)

    late = gather_quad(after(column_late, (near[1:], query, ordered, both_grads, bias)))
    fixed = (query, both_grads, bias, ordered, near)
    out_near, dq_near, away_near, *weight = attend(0, CUT, *fixed, near, n_batch, None)
    out_late, dq_late, away_late, kept, sent = attend(
        CUT, half - CUT, *fixed, late, n_batch, weight
    )

    back_near = swap(away_near, "hist", QUAD)
    back_late = swap(away_late, "hist", QUAD)
    sent = after(sent, back_near)
    kept = kept.reshape(QUAD, n_hist // QUAD, share, wide)
    sent = sent.reshape(n_batch - 1, QUAD, n_hist // QUAD, share, wide)
    total = kept
    for index in range(1, n_batch):
        total = total + swap(sent[index - 1], "batch", index).astype(F32)
    parts = [swap(total[index].astype(BF16), "hist", index) for index in range(1, QUAD)]
    back_late = after(back_late, parts[0])
    level = total[0]
    for part in parts:
        level = level + part.astype(F32)

    def join(index):
        own = [(out_near, dq_near)[index], (out_late, dq_late)[index]]
        back = [back_near[index], back_late[index]]
        return jnp.where(
            side == 0, jnp.concatenate(own + back, axis=1), jnp.concatenate(back + own, axis=1)
        )

    attended = join(0)
    d_targets = lax.dot_general(
        join(1), w_query, (((1,), (1,)), ((), ())), preferred_element_type=F32
    ).astype(BF16)
    level = after(level, (attended, d_targets))

    mask = n_hist // QUAD
    while mask > PAIR:
        mask //= 2
        level = level[:mask] + swap(level[mask:].astype(BF16), "hist", QUAD * mask).astype(F32)
    other = swap(level[1].astype(BF16), "hist", QUAD).astype(F32)
    d_query_weight = jnp.where(
        side == 0,
        jnp.concatenate([level[0], other], axis=1),
        jnp.concatenate([other, level[0]], axis=1),
    )
    return (attended[None], d_targets[None], d_query_weight)


def solution(mesh):
    in_specs = (
        P("batch", "hist", None),
        P(),
        P("batch", "hist", None),
        P("batch", "hist", None),
        P("batch", None, None),
        P("batch"),
        P("batch", "hist", None),
    )
    out_specs = (P("batch", "hist", None), P("batch", "hist", None), P(("hist", "batch"), None))
    return jax.shard_map(shards, mesh=mesh, in_specs=in_specs, out_specs=out_specs, check_vma=False)
```

```python
import functools

import jax
import jax.numpy as jnp
from jax import lax
from jax.experimental import pallas as pl
from jax.experimental.pallas import tpu as pltpu
from jax.sharding import PartitionSpec as P

BLK = 64
LANES = 128
TILE = 16
QUAD = 4
PAIR = 2
DEAD = -1e30
VMEM_LIMIT = 60 * 1024 * 1024
CUT = 2
STEP = 256
F32 = jnp.float32
BF16 = jnp.bfloat16


def swap(array, axis, mask):
    size = lax.axis_size(axis)
    return lax.ppermute(array, axis, [(i, i ^ mask) for i in range(size)])


def after(array, other):
    return lax.optimization_barrier((array, other))[0]


def select_kernel(cut, blocks_ref, lengths_ref, keys_ref, values_ref, *outs):
    heads, topk = blocks_ref.shape[1:]
    rows, width = keys_ref.shape[1:]
    half = heads // PAIR
    head_dim = width // heads
    blk_dev = rows // BLK
    rank = lax.axis_index("hist")
    side = (rank // QUAD) % PAIR
    length = lengths_ref[0]
    count = half * blk_dev
    room = -(-count // TILE) * TILE
    keep_near, keep_late, send_near, send_all = outs
    near_rows = keep_near.shape[0]
    sides = (
        (side * half, ((keep_near, 0),), ((keep_late, 0),)),
        ((1 - side) * half, ((send_near, 0), (send_all, 0)), ((send_all, near_rows),)),
    )
    for first, near, late in sides:
        for index in range(half):
            head = first + index
            local = jnp.int32(0)
            for entry in range(topk):
                block = blocks_ref[0, head, entry] - rank * blk_dev
                local = jnp.where((block >= 0) & (block < blk_dev), block, local)
            low = pl.multiple_of(local * BLK, BLK)
            at = (index - (cut if index >= cut else 0)) * BLK
            columns = pl.ds(pl.multiple_of(head * head_dim, head_dim), head_dim)
            key = keys_ref[0, pl.ds(low, BLK), columns]
            value = values_ref[0, pl.ds(low, BLK), columns]
            for out, base in late if index >= cut else near:
                out[base + at : base + at + BLK, :head_dim] = key
                out[base + at : base + at + BLK, head_dim:] = value
        span = pl.ds(pl.multiple_of(first * head_dim, head_dim), half * head_dim)
        for source, low in ((keys_ref, 0), (values_ref, head_dim)):
            totals = []
            for block in range(blk_dev):
                part = source[0, block * BLK : (block + 1) * BLK, span].astype(F32)
                spot = lax.broadcasted_iota(jnp.int32, part.shape, 0) + (rank * rows + block * BLK)
                part = jnp.where(spot < length, part, 0.0)
                totals.append(jnp.sum(part, axis=0, keepdims=True) * BLK ** (-0.5))
            lines = [
                totals[block][:, index * head_dim : (index + 1) * head_dim]
                for index in range(half)
                for block in range(blk_dev)
            ]
            lines.append(jnp.zeros((room - count, head_dim), F32))
            summary = jnp.concatenate(lines, axis=0).astype(BF16)
            for out, _ in near:
                out[cut * BLK : cut * BLK + room, low : low + head_dim] = summary


def attend_kernel(pieces, fine_width, scale, *refs):
    query_ref, grad_ref, bias_ref, ordered_ref = refs[:4]
    piece_refs = refs[4 : 4 + 2 * pieces]
    out_ref, dq_ref, away_ref, keep_ref, send_ref = refs[-5:]
    head_dim = query_ref.shape[1]
    keys = jnp.concatenate(
        [r[:, :, :head_dim].reshape(-1, head_dim) for r in piece_refs], axis=0
    )
    values = jnp.concatenate(
        [r[:, :, head_dim:].reshape(-1, head_dim) for r in piece_refs], axis=0
    )
    bias = bias_ref[0]
    cols = (slice(0, fine_width), slice(fine_width, keys.shape[0]))
    rows = out_ref.shape[0]
    step = min(STEP, rows)
    contract = (((1,), (1,)), ((), ()))
    d_queries = []
    places = ((out_ref, dq_ref, 0), (away_ref.at[0], away_ref.at[1], rows))
    for out_part, dq_part, base in places:
        for low in range(0, rows, step):
            query = query_ref[base + low : base + low + step, :]
            grad = grad_ref[base + low : base + low + step, :]
            scores = lax.dot_general(query, keys, contract, preferred_element_type=F32) * scale + bias
            d_probs = lax.dot_general(grad, values, contract, preferred_element_type=F32)
            probs_parts = []
            d_parts = []
            for part in cols:
                score = scores[:, part]
                expo = jnp.exp(score - jnp.max(score, axis=1, keepdims=True))
                probs = expo * (1.0 / jnp.sum(expo, axis=1, keepdims=True))
                d_prob = d_probs[:, part]
                delta = jnp.sum(probs * d_prob, axis=1, keepdims=True)
                probs_parts.append(probs.astype(BF16))
                d_parts.append((probs * (d_prob - delta)).astype(BF16))
            out = jnp.dot(jnp.concatenate(probs_parts, axis=1), values, preferred_element_type=F32)
            d_query = jnp.dot(jnp.concatenate(d_parts, axis=1), keys, preferred_element_type=F32)
            d_query = (d_query * scale).astype(BF16)
            out_part[low : low + step, :] = out.astype(BF16)
            dq_part[low : low + step, :] = d_query
            d_queries.append(d_query)
    weight = jnp.dot(
        ordered_ref[...], jnp.concatenate(d_queries, axis=0), preferred_element_type=F32
    )
    kept = keep_ref.shape[0]
    keep_ref[...] = weight[:kept]
    send_ref[...] = weight[kept:].astype(BF16)


def attend(first, count, query, grad, bias, ordered, summaries, pieces, share, earlier):
    rows, width = query.shape
    half = bias.shape[0]
    head_dim = width // half
    fine_width = sum(p.shape[0] for p in pieces) * BLK
    room = (bias.shape[-1] - fine_width) // sum(p.shape[0] for p in pieces)
    depth = ordered.shape[0]
    kept = depth // share
    in_specs = [
        pl.BlockSpec((rows, head_dim), lambda i: (0, first + i)),
        pl.BlockSpec((rows, head_dim), lambda i: (0, first + i)),
        pl.BlockSpec((1,) + bias.shape[1:], lambda i: (first + i, 0, 0)),
        pl.BlockSpec(ordered.shape, lambda i: (0, 0)),
    ]
    in_specs += [
        pl.BlockSpec((p.shape[0], BLK, 2 * head_dim), lambda i: (0, i, 0)) for p in pieces
    ]
    in_specs += [
        pl.BlockSpec((p.shape[0], room, 2 * head_dim), lambda i: (0, CUT * BLK // room, 0))
        for p in summaries
    ]
    args = [query, grad, bias, ordered, *pieces, *summaries]
    aliases = {}
    if earlier is not None:
        aliases = {len(args) + i: 3 + i for i in range(len(earlier))}
        args += list(earlier)
        in_specs += [pl.BlockSpec(memory_space=pl.ANY)] * len(earlier)
    own = jax.ShapeDtypeStruct((rows // PAIR, count * head_dim), BF16)
    own_spec = pl.BlockSpec((rows // PAIR, head_dim), lambda i: (0, i))
    columns = bias.shape[-1]
    return pl.pallas_call(
        functools.partial(attend_kernel, len(pieces), fine_width, head_dim ** (-0.5)),
        grid=(count,),
        in_specs=in_specs,
        out_specs=(
            own_spec,
            own_spec,
            pl.BlockSpec((2, rows // PAIR, head_dim), lambda i: (0, 0, i)),
            pl.BlockSpec((kept, head_dim), lambda i: (0, first + i)),
            pl.BlockSpec((depth - kept, head_dim), lambda i: (0, first + i)),
        ),
        out_shape=(
            own,
            own,
            jax.ShapeDtypeStruct((2,) + own.shape, BF16),
            jax.ShapeDtypeStruct((kept, width), F32),
            jax.ShapeDtypeStruct((depth - kept, width), BF16),
        ),
        input_output_aliases=aliases,
        compiler_params=pltpu.CompilerParams(vmem_limit_bytes=VMEM_LIMIT),
        cost_estimate=pl.CostEstimate(
            flops=8 * count * rows * columns * head_dim,
            bytes_accessed=count * (columns * 512 + rows * head_dim * 8),
            transcendentals=count * rows * columns,
        ),
        name="attend",
    )(*args)


def gather_quad(column):
    return [column] + [swap(column, "hist", mask) for mask in range(1, QUAD)]


def shards(targets, w_query, keys, values, blocks, lengths, d_attended):
    heads = blocks.shape[1]
    local_rows, width = keys.shape[1:]
    head_dim = width // heads
    blk_dev = local_rows // BLK
    n_hist = lax.axis_size("hist")
    n_batch = lax.axis_size("batch")
    rank = lax.axis_index("hist")
    lane = lax.axis_index("batch")
    rows = targets.shape[1]
    depth = targets.shape[2]
    half = heads // PAIR
    side = (rank // QUAD) % PAIR
    wide = half * head_dim
    count = half * blk_dev
    room = -(-count // TILE) * TILE
    near_rows = CUT * BLK + room
    late_rows = (half - CUT) * BLK
    keep_near, keep_late, send_near, send = pl.pallas_call(
        functools.partial(select_kernel, CUT),
        in_specs=[
            pl.BlockSpec(memory_space=pltpu.SMEM),
            pl.BlockSpec(memory_space=pltpu.SMEM),
            pl.BlockSpec(memory_space=pltpu.VMEM),
            pl.BlockSpec(memory_space=pltpu.VMEM),
        ],
        out_specs=[pl.BlockSpec(memory_space=pltpu.VMEM)] * 4,
        out_shape=[
            jax.ShapeDtypeStruct((size, 2 * head_dim), BF16)
            for size in (near_rows, late_rows, near_rows, near_rows + late_rows)
        ],
        name="select",
    )(blocks, lengths, keys, values)
    came = swap(send, "hist", QUAD)
    column_near = jnp.stack(
        [keep_near, came[:near_rows]]
        + [
            swap((keep_near, send_near)[k % PAIR], "hist", QUAD * k)
            for k in range(PAIR, n_hist // QUAD)
        ]
    )
    near = gather_quad(column_near)
    pair_late = after(jnp.stack([keep_late, came[near_rows:]]), column_near)
    column_late = jnp.concatenate(
        [pair_late]
        + [swap(pair_late, "hist", QUAD * k) for k in range(PAIR, n_hist // QUAD, PAIR)]
    )

    grad = d_attended[0]
    grad_keep = lax.dynamic_slice_in_dim(grad, side * wide, wide, 1)
    grad_send = lax.dynamic_slice_in_dim(grad, (1 - side) * wide, wide, 1)
    theirs = swap(jnp.concatenate([targets[0], grad_send]), "hist", QUAD)
    their_targets, their_grads = theirs[:rows], theirs[rows:]
    both_targets = jnp.concatenate([targets[0], their_targets], axis=0)
    both_grads = jnp.concatenate([grad_keep, their_grads], axis=0)
    weights = lax.dynamic_slice_in_dim(w_query, side * wide, wide, 1)
    query = jnp.dot(both_targets, weights, preferred_element_type=F32).astype(BF16)

    masks = jnp.asarray([q + QUAD * k for q in range(QUAD) for k in range(n_hist // QUAD)], jnp.int32)
    source = rank ^ masks
    lists = lax.dynamic_slice_in_dim(after(blocks, column_near)[0], side * half, half, 0)
    listed = jnp.max(
        jnp.where((lists // blk_dev)[:, :, None] == source[None, None, :], lists[:, :, None], -1),
        axis=1,
    )
    spots = jnp.arange(BLK, dtype=jnp.int32)
    live = (listed[:, :, None] >= 0) & (listed[:, :, None] * BLK + spots < lengths[0])
    fine_bias = jnp.where(live, 0.0, DEAD).astype(F32).reshape(half, -1)
    line = jnp.arange(room, dtype=jnp.int32)
    names = source[:, None] * blk_dev + line[None, :] % blk_dev
    own_line = (line // blk_dev)[None, :] == jnp.arange(half, dtype=jnp.int32)[:, None]
    coarse_live = own_line[:, None, :] & (names * BLK < lengths[0])[None]
    coarse_bias = jnp.where(coarse_live, 0.0, DEAD).astype(F32).reshape(half, -1)
    bias = jnp.concatenate([fine_bias, coarse_bias], axis=1)[:, None, :]

    places = (
        (rank ^ masks)[None, :] * n_batch + (lane ^ jnp.arange(n_batch, dtype=jnp.int32))[:, None]
    ).reshape(-1)
    share = depth // (n_hist * n_batch)
    chosen = (places[:, None] * share + jnp.arange(share, dtype=jnp.int32)).reshape(-1)
    shuffle = (chosen[:, None] == jnp.arange(depth, dtype=jnp.int32)[None, :]).astype(BF16)
    ordered = lax.dot_general(
        shuffle, both_targets, (((1,), (1,)), ((), ())), preferred_element_type=F32
    ).astype(BF16)

    late = gather_quad(after(column_late, (near[1:], query, ordered, both_grads, bias)))
    fixed = (query, both_grads, bias, ordered, near)
    out_near, dq_near, away_near, *weight = attend(0, CUT, *fixed, near, n_batch, None)
    out_late, dq_late, away_late, kept, sent = attend(
        CUT, half - CUT, *fixed, late, n_batch, weight
    )

    back_near = swap(away_near, "hist", QUAD)
    back_late = swap(away_late, "hist", QUAD)
    sent = after(sent, back_near)
    kept = kept.reshape(QUAD, n_hist // QUAD, share, wide)
    sent = sent.reshape(n_batch - 1, QUAD, n_hist // QUAD, share, wide)
    total = kept
    for index in range(1, n_batch):
        total = total + swap(sent[index - 1], "batch", index).astype(F32)
    parts = [swap(total[index].astype(BF16), "hist", index) for index in range(1, QUAD)]
    back_late = after(back_late, parts[0])
    level = total[0]
    for part in parts:
        level = level + part.astype(F32)

    def join(index):
        own = [(out_near, dq_near)[index], (out_late, dq_late)[index]]
        back = [back_near[index], back_late[index]]
        return jnp.where(
            side == 0, jnp.concatenate(own + back, axis=1), jnp.concatenate(back + own, axis=1)
        )

    attended = join(0)
    d_targets = lax.dot_general(
        join(1), w_query, (((1,), (1,)), ((), ())), preferred_element_type=F32
    ).astype(BF16)
    level = after(level, (attended, d_targets))

    sums = [level[0], None]
    for index in range(1, n_hist // QUAD):
        got = swap(level[index].astype(BF16), "hist", QUAD * index).astype(F32)
        sums[index % PAIR] = got if sums[index % PAIR] is None else sums[index % PAIR] + got
    d_query_weight = jnp.where(
        side == 0, jnp.concatenate(sums, axis=1), jnp.concatenate(sums[::-1], axis=1)
    )
    return (attended[None], d_targets[None], d_query_weight)


def solution(mesh):
    in_specs = (
        P("batch", "hist", None),
        P(),
        P("batch", "hist", None),
        P("batch", "hist", None),
        P("batch", None, None),
        P("batch"),
        P("batch", "hist", None),
    )
    out_specs = (P("batch", "hist", None), P("batch", "hist", None), P(("hist", "batch"), None))
    return jax.shard_map(shards, mesh=mesh, in_specs=in_specs, out_specs=out_specs, check_vma=False)
```

```python
import functools

import jax
import jax.numpy as jnp
from jax import lax
from jax.experimental import pallas as pl
from jax.experimental.pallas import tpu as pltpu
from jax.sharding import PartitionSpec as P

BLK = 64
LANES = 128
TILE = 16
QUAD = 4
PAIR = 2
DEAD = -1e30
VMEM_LIMIT = 60 * 1024 * 1024
CUT = 2
F32 = jnp.float32
BF16 = jnp.bfloat16


def swap(array, axis, mask):
    size = lax.axis_size(axis)
    return lax.ppermute(array, axis, [(i, i ^ mask) for i in range(size)])


def after(array, other):
    return lax.optimization_barrier((array, other))[0]


def select_kernel(cut, blocks_ref, lengths_ref, keys_ref, values_ref, *outs):
    heads, topk = blocks_ref.shape[1:]
    rows, width = keys_ref.shape[1:]
    half = heads // PAIR
    head_dim = width // heads
    blk_dev = rows // BLK
    rank = lax.axis_index("hist")
    side = (rank // QUAD) % PAIR
    length = lengths_ref[0]
    count = half * blk_dev
    room = -(-count // TILE) * TILE
    keep_near, keep_late, send_near, send_all = outs
    near_rows = keep_near.shape[0]
    sides = (
        (side * half, ((keep_near, 0),), ((keep_late, 0),)),
        ((1 - side) * half, ((send_near, 0), (send_all, 0)), ((send_all, near_rows),)),
    )
    for first, near, late in sides:
        for index in range(half):
            head = first + index
            local = jnp.int32(0)
            for entry in range(topk):
                block = blocks_ref[0, head, entry] - rank * blk_dev
                local = jnp.where((block >= 0) & (block < blk_dev), block, local)
            low = pl.multiple_of(local * BLK, BLK)
            at = (index - (cut if index >= cut else 0)) * BLK
            columns = pl.ds(pl.multiple_of(head * head_dim, head_dim), head_dim)
            key = keys_ref[0, pl.ds(low, BLK), columns]
            value = values_ref[0, pl.ds(low, BLK), columns]
            for out, base in late if index >= cut else near:
                out[base + at : base + at + BLK, :head_dim] = key
                out[base + at : base + at + BLK, head_dim:] = value
        span = pl.ds(pl.multiple_of(first * head_dim, head_dim), half * head_dim)
        for source, low in ((keys_ref, 0), (values_ref, head_dim)):
            totals = []
            for block in range(blk_dev):
                part = source[0, block * BLK : (block + 1) * BLK, span].astype(F32)
                spot = lax.broadcasted_iota(jnp.int32, part.shape, 0) + (rank * rows + block * BLK)
                part = jnp.where(spot < length, part, 0.0)
                totals.append(jnp.sum(part, axis=0, keepdims=True) * BLK ** (-0.5))
            lines = [
                totals[block][:, index * head_dim : (index + 1) * head_dim]
                for index in range(half)
                for block in range(blk_dev)
            ]
            lines.append(jnp.zeros((room - count, head_dim), F32))
            summary = jnp.concatenate(lines, axis=0).astype(BF16)
            for out, _ in near:
                out[cut * BLK : cut * BLK + room, low : low + head_dim] = summary


def attend_kernel(pieces, fine_width, scale, *refs):
    bias_ref = refs[0]
    inputs = (refs[1:4], refs[4:7])
    piece_refs = refs[7 : 7 + pieces]
    out_ref, dq_ref, away_ref, keep_ref, send_ref = refs[-5:]
    head_dim = out_ref.shape[1]
    keys = jnp.concatenate(
        [r[:, :, :head_dim].reshape(-1, head_dim) for r in piece_refs], axis=0
    )
    values = jnp.concatenate(
        [r[:, :, head_dim:].reshape(-1, head_dim) for r in piece_refs], axis=0
    )
    bias = bias_ref[0]
    cols = (slice(0, fine_width), slice(fine_width, keys.shape[0]))
    contract = (((1,), (1,)), ((), ()))
    weight = 0.0
    places = ((out_ref, dq_ref), (away_ref.at[0], away_ref.at[1]))
    for (query_ref, grad_ref, ordered_ref), (out_part, dq_part) in zip(inputs, places):
        scores = lax.dot_general(query_ref[...], keys, contract, preferred_element_type=F32)
        scores = scores * scale + bias
        d_probs = lax.dot_general(grad_ref[...], values, contract, preferred_element_type=F32)
        probs_parts = []
        d_parts = []
        for part in cols:
            score = scores[:, part]
            expo = jnp.exp(score - jnp.max(score, axis=1, keepdims=True))
            probs = expo * (1.0 / jnp.sum(expo, axis=1, keepdims=True))
            d_prob = d_probs[:, part]
            delta = jnp.sum(probs * d_prob, axis=1, keepdims=True)
            probs_parts.append(probs.astype(BF16))
            d_parts.append((probs * (d_prob - delta)).astype(BF16))
        out = jnp.dot(jnp.concatenate(probs_parts, axis=1), values, preferred_element_type=F32)
        d_query = jnp.dot(jnp.concatenate(d_parts, axis=1), keys, preferred_element_type=F32)
        d_query = (d_query * scale).astype(BF16)
        out_part[...] = out.astype(BF16)
        dq_part[...] = d_query
        weight = weight + jnp.dot(ordered_ref[...], d_query, preferred_element_type=F32)
    kept = keep_ref.shape[0]
    keep_ref[...] = weight[:kept]
    send_ref[...] = weight[kept:].astype(BF16)


def attend(first, count, bias, own_side, their_side, summaries, pieces, share, earlier):
    rows = own_side[0].shape[0]
    depth = own_side[2].shape[0]
    half = bias.shape[0]
    width = own_side[0].shape[1]
    head_dim = width // half
    fine_width = sum(p.shape[0] for p in pieces) * BLK
    room = (bias.shape[-1] - fine_width) // sum(p.shape[0] for p in pieces)
    kept = depth // share
    in_specs = [pl.BlockSpec((1,) + bias.shape[1:], lambda i: (first + i, 0, 0))]
    for at in (0, own_side[1].shape[0] // rows - 1), (0, their_side[1].shape[0] // rows - 1):
        in_specs += [
            pl.BlockSpec((rows, head_dim), lambda i, at=at[0]: (at, first + i)),
            pl.BlockSpec((rows, head_dim), lambda i, at=at[1]: (at, first + i)),
            pl.BlockSpec((depth, rows), lambda i: (0, 0)),
        ]
    in_specs += [
        pl.BlockSpec((p.shape[0], BLK, 2 * head_dim), lambda i: (0, i, 0)) for p in pieces
    ]
    in_specs += [
        pl.BlockSpec((p.shape[0], room, 2 * head_dim), lambda i: (0, CUT * BLK // room, 0))
        for p in summaries
    ]
    args = [bias, *own_side, *their_side, *pieces, *summaries]
    aliases = {}
    if earlier is not None:
        aliases = {len(args) + i: 3 + i for i in range(len(earlier))}
        args += list(earlier)
        in_specs += [pl.BlockSpec(memory_space=pl.ANY)] * len(earlier)
    own = jax.ShapeDtypeStruct((rows, count * head_dim), BF16)
    own_spec = pl.BlockSpec((rows, head_dim), lambda i: (0, i))
    columns = bias.shape[-1]
    return pl.pallas_call(
        functools.partial(attend_kernel, len(pieces) + len(summaries), fine_width, head_dim ** (-0.5)),
        grid=(count,),
        in_specs=in_specs,
        out_specs=(
            own_spec,
            own_spec,
            pl.BlockSpec((2, rows, head_dim), lambda i: (0, 0, i)),
            pl.BlockSpec((kept, head_dim), lambda i: (0, first + i)),
            pl.BlockSpec((depth - kept, head_dim), lambda i: (0, first + i)),
        ),
        out_shape=(
            own,
            own,
            jax.ShapeDtypeStruct((2,) + own.shape, BF16),
            jax.ShapeDtypeStruct((kept, width), F32),
            jax.ShapeDtypeStruct((depth - kept, width), BF16),
        ),
        input_output_aliases=aliases,
        compiler_params=pltpu.CompilerParams(vmem_limit_bytes=VMEM_LIMIT),
        cost_estimate=pl.CostEstimate(
            flops=16 * count * rows * columns * head_dim,
            bytes_accessed=count * (columns * 512 + rows * head_dim * 8),
            transcendentals=2 * count * rows * columns,
        ),
        name="attend",
    )(*args)


def gather_quad(column):
    return [column] + [swap(column, "hist", mask) for mask in range(1, QUAD)]


def shards(targets, w_query, keys, values, blocks, lengths, d_attended):
    heads = blocks.shape[1]
    local_rows, width = keys.shape[1:]
    head_dim = width // heads
    blk_dev = local_rows // BLK
    n_hist = lax.axis_size("hist")
    n_batch = lax.axis_size("batch")
    rank = lax.axis_index("hist")
    lane = lax.axis_index("batch")
    rows = targets.shape[1]
    depth = targets.shape[2]
    half = heads // PAIR
    side = (rank // QUAD) % PAIR
    wide = half * head_dim
    count = half * blk_dev
    room = -(-count // TILE) * TILE
    near_rows = CUT * BLK + room
    late_rows = (half - CUT) * BLK
    keep_near, keep_late, send_near, send = pl.pallas_call(
        functools.partial(select_kernel, CUT),
        in_specs=[
            pl.BlockSpec(memory_space=pltpu.SMEM),
            pl.BlockSpec(memory_space=pltpu.SMEM),
            pl.BlockSpec(memory_space=pltpu.VMEM),
            pl.BlockSpec(memory_space=pltpu.VMEM),
        ],
        out_specs=[pl.BlockSpec(memory_space=pltpu.VMEM)] * 4,
        out_shape=[
            jax.ShapeDtypeStruct((size, 2 * head_dim), BF16)
            for size in (near_rows, late_rows, near_rows, near_rows + late_rows)
        ],
        name="select",
    )(blocks, lengths, keys, values)
    came = swap(send, "hist", QUAD)
    column_near = jnp.stack(
        [keep_near, came[:near_rows]]
        + [
            swap((keep_near, send_near)[k % PAIR], "hist", QUAD * k)
            for k in range(PAIR, n_hist // QUAD)
        ]
    )
    near = gather_quad(column_near)
    pair_late = after(jnp.stack([keep_late, came[near_rows:]]), column_near)
    column_late = jnp.concatenate(
        [pair_late]
        + [swap(pair_late, "hist", QUAD * k) for k in range(PAIR, n_hist // QUAD, PAIR)]
    )

    grad = d_attended[0]
    grad_keep = lax.dynamic_slice_in_dim(grad, side * wide, wide, 1)
    grad_send = lax.dynamic_slice_in_dim(grad, (1 - side) * wide, wide, 1)
    theirs = swap(jnp.concatenate([targets[0], grad_send]), "hist", QUAD)
    weights = lax.dynamic_slice_in_dim(w_query, side * wide, wide, 1)

    def project(part):
        return jnp.dot(part, weights, preferred_element_type=F32).astype(BF16)

    masks = jnp.asarray([q + QUAD * k for q in range(QUAD) for k in range(n_hist // QUAD)], jnp.int32)
    source = rank ^ masks
    lists = lax.dynamic_slice_in_dim(blocks[0], side * half, half, 0)
    listed = jnp.max(
        jnp.where((lists // blk_dev)[:, :, None] == source[None, None, :], lists[:, :, None], -1),
        axis=1,
    )
    spots = jnp.arange(BLK, dtype=jnp.int32)
    live = (listed[:, :, None] >= 0) & (listed[:, :, None] * BLK + spots < lengths[0])
    fine_bias = jnp.where(live, 0.0, DEAD).astype(F32).reshape(half, -1)
    line = jnp.arange(room, dtype=jnp.int32)
    names = source[:, None] * blk_dev + line[None, :] % blk_dev
    own_line = (line // blk_dev)[None, :] == jnp.arange(half, dtype=jnp.int32)[:, None]
    coarse_live = own_line[:, None, :] & (names * BLK < lengths[0])[None]
    coarse_bias = jnp.where(coarse_live, 0.0, DEAD).astype(F32).reshape(half, -1)
    fine_bias = after(fine_bias, column_near)
    bias = jnp.concatenate([fine_bias, coarse_bias], axis=1)[:, None, :]

    places = (
        (rank ^ masks)[None, :] * n_batch + (lane ^ jnp.arange(n_batch, dtype=jnp.int32))[:, None]
    ).reshape(-1)
    share = depth // (n_hist * n_batch)
    chosen = (places[:, None] * share + jnp.arange(share, dtype=jnp.int32)).reshape(-1)
    shuffle = (chosen[:, None] == jnp.arange(depth, dtype=jnp.int32)[None, :]).astype(BF16)

    def reorder(part):
        product = lax.dot_general(
            shuffle, part, (((1,), (1,)), ((), ())), preferred_element_type=F32
        )
        return product.astype(BF16)

    own_side = (project(targets[0]), grad_keep, reorder(targets[0]))
    their_side = (project(theirs[:rows]), theirs, reorder(theirs[:rows]))
    late = gather_quad(after(column_late, theirs))
    fixed = (bias, own_side, their_side, near)
    out_near, dq_near, away_near, *weight = attend(0, CUT, *fixed, near, n_batch, None)
    out_late, dq_late, away_late, kept, sent = attend(
        CUT, half - CUT, *fixed, late, n_batch, weight
    )

    back_near = swap(away_near, "hist", QUAD)
    back_late = swap(away_late, "hist", QUAD)
    sent = after(sent, back_near)
    kept = kept.reshape(QUAD, n_hist // QUAD, share, wide)
    sent = sent.reshape(n_batch - 1, QUAD, n_hist // QUAD, share, wide)
    total = kept
    for index in range(1, n_batch):
        total = total + swap(sent[index - 1], "batch", index).astype(F32)
    parts = [swap(total[index].astype(BF16), "hist", index) for index in range(1, QUAD)]
    back_late = after(back_late, parts[0])
    level = total[0]
    for part in parts:
        level = level + part.astype(F32)

    def join(index):
        own = [(out_near, dq_near)[index], (out_late, dq_late)[index]]
        back = [back_near[index], back_late[index]]
        return jnp.where(
            side == 0, jnp.concatenate(own + back, axis=1), jnp.concatenate(back + own, axis=1)
        )

    attended = join(0)
    d_targets = lax.dot_general(
        join(1), w_query, (((1,), (1,)), ((), ())), preferred_element_type=F32
    ).astype(BF16)
    level = after(level, (attended, d_targets))

    sums = [level[0], None]
    for index in range(1, n_hist // QUAD):
        got = swap(level[index].astype(BF16), "hist", QUAD * index).astype(F32)
        sums[index % PAIR] = got if sums[index % PAIR] is None else sums[index % PAIR] + got
    d_query_weight = jnp.where(
        side == 0, jnp.concatenate(sums, axis=1), jnp.concatenate(sums[::-1], axis=1)
    )
    return (attended[None], d_targets[None], d_query_weight)


def solution(mesh):
    in_specs = (
        P("batch", "hist", None),
        P(),
        P("batch", "hist", None),
        P("batch", "hist", None),
        P("batch", None, None),
        P("batch"),
        P("batch", "hist", None),
    )
    out_specs = (P("batch", "hist", None), P("batch", "hist", None), P(("hist", "batch"), None))
    return jax.shard_map(shards, mesh=mesh, in_specs=in_specs, out_specs=out_specs, check_vma=False)
```

```python
import functools

import jax
import jax.numpy as jnp
from jax import lax
from jax.experimental import pallas as pl
from jax.experimental.pallas import tpu as pltpu
from jax.sharding import PartitionSpec as P

BLK = 64
LANES = 128
TILE = 16
QUAD = 4
PAIR = 2
DEAD = -1e30
VMEM_LIMIT = 60 * 1024 * 1024
VMEM_SOURCE = 1280 * 1024
CUT = 2
F32 = jnp.float32
BF16 = jnp.bfloat16


def swap(array, axis, mask):
    size = lax.axis_size(axis)
    return lax.ppermute(array, axis, [(i, i ^ mask) for i in range(size)])


def after(array, other):
    return lax.optimization_barrier((array, other))[0]


def select_kernel(cut, blocks_ref, lengths_ref, keys_ref, values_ref, *outs):
    heads, topk = blocks_ref.shape[1:]
    rows, width = keys_ref.shape[1:]
    half = heads // PAIR
    head_dim = width // heads
    blk_dev = rows // BLK
    rank = lax.axis_index("hist")
    side = (rank // QUAD) % PAIR
    length = lengths_ref[0]
    count = half * blk_dev
    room = -(-count // TILE) * TILE
    keep_near, keep_late, send_near, send_all = outs
    near_rows = keep_near.shape[0]
    sides = (
        (side * half, ((keep_near, 0),), ((keep_late, 0),)),
        ((1 - side) * half, ((send_near, 0), (send_all, 0)), ((send_all, near_rows),)),
    )
    for first, near, late in sides:
        for index in range(half):
            head = first + index
            local = jnp.int32(0)
            for entry in range(topk):
                block = blocks_ref[0, head, entry] - rank * blk_dev
                local = jnp.where((block >= 0) & (block < blk_dev), block, local)
            low = pl.multiple_of(local * BLK, BLK)
            at = (index - (cut if index >= cut else 0)) * BLK
            columns = pl.ds(pl.multiple_of(head * head_dim, head_dim), head_dim)
            key = keys_ref[0, pl.ds(low, BLK), columns]
            value = values_ref[0, pl.ds(low, BLK), columns]
            for out, base in late if index >= cut else near:
                out[base + at : base + at + BLK, :head_dim] = key
                out[base + at : base + at + BLK, head_dim:] = value
        span = pl.ds(pl.multiple_of(first * head_dim, head_dim), half * head_dim)
        for source, low in ((keys_ref, 0), (values_ref, head_dim)):
            totals = []
            for block in range(blk_dev):
                part = source[0, block * BLK : (block + 1) * BLK, span].astype(F32)
                spot = lax.broadcasted_iota(jnp.int32, part.shape, 0) + (rank * rows + block * BLK)
                part = jnp.where(spot < length, part, 0.0)
                totals.append(jnp.sum(part, axis=0, keepdims=True) * BLK ** (-0.5))
            lines = [
                totals[block][:, index * head_dim : (index + 1) * head_dim]
                for index in range(half)
                for block in range(blk_dev)
            ]
            lines.append(jnp.zeros((room - count, head_dim), F32))
            summary = jnp.concatenate(lines, axis=0).astype(BF16)
            for out, _ in near:
                out[cut * BLK : cut * BLK + room, low : low + head_dim] = summary


def attend_kernel(pieces, fine_width, scale, *refs):
    bias_ref = refs[0]
    inputs = (refs[1:3], refs[4:6])
    own_order, their_order = refs[3], refs[6]
    piece_refs = refs[7 : 7 + pieces]
    out_ref, dq_ref, away_ref, keep_ref, send_ref = refs[-5:]
    head_dim = out_ref.shape[1]
    keys = jnp.concatenate(
        [r[:, :, :head_dim].reshape(-1, head_dim) for r in piece_refs], axis=0
    )
    values = jnp.concatenate(
        [r[:, :, head_dim:].reshape(-1, head_dim) for r in piece_refs], axis=0
    )
    bias = bias_ref[0]
    cols = (slice(0, fine_width), slice(fine_width, keys.shape[0]))
    contract = (((1,), (1,)), ((), ()))
    query, grad = (jnp.concatenate([own[...], their[...]]) for own, their in zip(*inputs))
    scores = lax.dot_general(query, keys, contract, preferred_element_type=F32) * scale + bias
    d_probs = lax.dot_general(grad, values, contract, preferred_element_type=F32)
    probs_parts = []
    d_parts = []
    for part in cols:
        score = scores[:, part]
        expo = jnp.exp(score - jnp.max(score, axis=1, keepdims=True))
        probs = expo * (1.0 / jnp.sum(expo, axis=1, keepdims=True))
        d_prob = d_probs[:, part]
        delta = jnp.sum(probs * d_prob, axis=1, keepdims=True)
        probs_parts.append(probs.astype(BF16))
        d_parts.append((probs * (d_prob - delta)).astype(BF16))
    out = jnp.dot(jnp.concatenate(probs_parts, axis=1), values, preferred_element_type=F32)
    d_query = jnp.dot(jnp.concatenate(d_parts, axis=1), keys, preferred_element_type=F32)
    out = out.astype(BF16)
    d_query = (d_query * scale).astype(BF16)
    rows = out_ref.shape[0]
    out_ref[...] = out[:rows]
    dq_ref[...] = d_query[:rows]
    away_ref[0] = out[rows:]
    away_ref[1] = d_query[rows:]
    weight = jnp.dot(own_order[...], d_query[:rows], preferred_element_type=F32)
    weight += jnp.dot(their_order[...], d_query[rows:], preferred_element_type=F32)
    kept = keep_ref.shape[0]
    keep_ref[...] = weight[:kept]
    send_ref[...] = weight[kept:].astype(BF16)


def attend(first, count, bias, own_side, their_side, summaries, pieces, share, earlier):
    rows = own_side[0].shape[0]
    depth = own_side[2].shape[0]
    half = bias.shape[0]
    width = own_side[0].shape[1]
    head_dim = width // half
    fine_width = sum(p.shape[0] for p in pieces) * BLK
    room = (bias.shape[-1] - fine_width) // sum(p.shape[0] for p in pieces)
    kept = depth // share
    in_specs = [pl.BlockSpec((1,) + bias.shape[1:], lambda i: (first + i, 0, 0))]
    for at in (0, own_side[1].shape[0] // rows - 1), (0, their_side[1].shape[0] // rows - 1):
        in_specs += [
            pl.BlockSpec((rows, head_dim), lambda i, at=at[0]: (at, first + i)),
            pl.BlockSpec((rows, head_dim), lambda i, at=at[1]: (at, first + i)),
            pl.BlockSpec((depth, rows), lambda i: (0, 0)),
        ]
    in_specs += [
        pl.BlockSpec((p.shape[0], BLK, 2 * head_dim), lambda i: (0, i, 0)) for p in pieces
    ]
    in_specs += [
        pl.BlockSpec((p.shape[0], room, 2 * head_dim), lambda i: (0, CUT * BLK // room, 0))
        for p in summaries
    ]
    args = [bias, *own_side, *their_side, *pieces, *summaries]
    aliases = {}
    if earlier is not None:
        aliases = {len(args) + i: 3 + i for i in range(len(earlier))}
        args += list(earlier)
        in_specs += [pl.BlockSpec(memory_space=pl.ANY)] * len(earlier)
    own = jax.ShapeDtypeStruct((rows, count * head_dim), BF16)
    own_spec = pl.BlockSpec((rows, head_dim), lambda i: (0, i))
    columns = bias.shape[-1]
    return pl.pallas_call(
        functools.partial(attend_kernel, len(pieces) + len(summaries), fine_width, head_dim ** (-0.5)),
        grid=(count,),
        in_specs=in_specs,
        out_specs=(
            own_spec,
            own_spec,
            pl.BlockSpec((2, rows, head_dim), lambda i: (0, 0, i)),
            pl.BlockSpec((kept, head_dim), lambda i: (0, first + i)),
            pl.BlockSpec((depth - kept, head_dim), lambda i: (0, first + i)),
        ),
        out_shape=(
            own,
            own,
            jax.ShapeDtypeStruct((2,) + own.shape, BF16),
            jax.ShapeDtypeStruct((kept, width), F32),
            jax.ShapeDtypeStruct((depth - kept, width), BF16),
        ),
        input_output_aliases=aliases,
        compiler_params=pltpu.CompilerParams(
            vmem_limit_bytes=min(VMEM_LIMIT, sum(p.shape[0] for p in pieces) * VMEM_SOURCE)
        ),
        cost_estimate=pl.CostEstimate(
            flops=16 * count * rows * columns * head_dim,
            bytes_accessed=count * (columns * 512 + rows * head_dim * 8),
            transcendentals=2 * count * rows * columns,
        ),
        name="attend",
    )(*args)


def gather_quad(column):
    return [column] + [swap(column, "hist", mask) for mask in range(1, QUAD)]


def shards(targets, w_query, keys, values, blocks, lengths, d_attended):
    heads = blocks.shape[1]
    local_rows, width = keys.shape[1:]
    head_dim = width // heads
    blk_dev = local_rows // BLK
    n_hist = lax.axis_size("hist")
    n_batch = lax.axis_size("batch")
    rank = lax.axis_index("hist")
    lane = lax.axis_index("batch")
    rows = targets.shape[1]
    depth = targets.shape[2]
    half = heads // PAIR
    side = (rank // QUAD) % PAIR
    wide = half * head_dim
    count = half * blk_dev
    room = -(-count // TILE) * TILE
    near_rows = CUT * BLK + room
    late_rows = (half - CUT) * BLK
    keep_near, keep_late, send_near, send = pl.pallas_call(
        functools.partial(select_kernel, CUT),
        in_specs=[
            pl.BlockSpec(memory_space=pltpu.SMEM),
            pl.BlockSpec(memory_space=pltpu.SMEM),
            pl.BlockSpec(memory_space=pltpu.VMEM),
            pl.BlockSpec(memory_space=pltpu.VMEM),
        ],
        out_specs=[pl.BlockSpec(memory_space=pltpu.VMEM)] * 4,
        out_shape=[
            jax.ShapeDtypeStruct((size, 2 * head_dim), BF16)
            for size in (near_rows, late_rows, near_rows, near_rows + late_rows)
        ],
        name="select",
    )(blocks, lengths, keys, values)
    came = swap(send, "hist", QUAD)
    column_near = jnp.stack(
        [keep_near, came[:near_rows]]
        + [
            swap((keep_near, send_near)[k % PAIR], "hist", QUAD * k)
            for k in range(PAIR, n_hist // QUAD)
        ]
    )
    near = gather_quad(column_near)
    pair_late = after(jnp.stack([keep_late, came[near_rows:]]), column_near)
    column_late = jnp.concatenate(
        [pair_late]
        + [swap(pair_late, "hist", QUAD * k) for k in range(PAIR, n_hist // QUAD, PAIR)]
    )

    grad = d_attended[0]
    grad_keep = lax.dynamic_slice_in_dim(grad, side * wide, wide, 1)
    grad_send = lax.dynamic_slice_in_dim(grad, (1 - side) * wide, wide, 1)
    theirs = swap(jnp.concatenate([targets[0], grad_send]), "hist", QUAD)
    weights = lax.dynamic_slice_in_dim(w_query, side * wide, wide, 1)

    def project(part):
        return jnp.dot(part, weights, preferred_element_type=F32).astype(BF16)

    masks = jnp.asarray([q + QUAD * k for q in range(QUAD) for k in range(n_hist // QUAD)], jnp.int32)
    source = rank ^ masks
    lists = lax.dynamic_slice_in_dim(blocks[0], side * half, half, 0)
    listed = jnp.max(
        jnp.where((lists // blk_dev)[:, :, None] == source[None, None, :], lists[:, :, None], -1),
        axis=1,
    )
    spots = jnp.arange(BLK, dtype=jnp.int32)
    live = (listed[:, :, None] >= 0) & (listed[:, :, None] * BLK + spots < lengths[0])
    fine_bias = jnp.where(live, 0.0, DEAD).astype(F32).reshape(half, -1)
    line = jnp.arange(room, dtype=jnp.int32)
    names = source[:, None] * blk_dev + line[None, :] % blk_dev
    own_line = (line // blk_dev)[None, :] == jnp.arange(half, dtype=jnp.int32)[:, None]
    coarse_live = own_line[:, None, :] & (names * BLK < lengths[0])[None]
    coarse_bias = jnp.where(coarse_live, 0.0, DEAD).astype(F32).reshape(half, -1)
    fine_bias = after(fine_bias, column_near)
    bias = jnp.concatenate([fine_bias, coarse_bias], axis=1)[:, None, :]

    places = (
        (rank ^ masks)[None, :] * n_batch + (lane ^ jnp.arange(n_batch, dtype=jnp.int32))[:, None]
    ).reshape(-1)
    share = depth // (n_hist * n_batch)
    chosen = (places[:, None] * share + jnp.arange(share, dtype=jnp.int32)).reshape(-1)
    shuffle = (chosen[:, None] == jnp.arange(depth, dtype=jnp.int32)[None, :]).astype(BF16)

    def reorder(part):
        product = lax.dot_general(
            shuffle, part, (((1,), (1,)), ((), ())), preferred_element_type=F32
        )
        return product.astype(BF16)

    own_side = (project(targets[0]), grad_keep, reorder(targets[0]))
    their_side = (project(theirs[:rows]), theirs, reorder(theirs[:rows]))
    late = gather_quad(after(column_late, theirs))
    fixed = (bias, own_side, their_side, near)
    out_near, dq_near, away_near, *weight = attend(0, CUT, *fixed, near, n_batch, None)
    out_late, dq_late, away_late, kept, sent = attend(
        CUT, half - CUT, *fixed, late, n_batch, weight
    )

    back_near = swap(away_near, "hist", QUAD)
    back_late = swap(away_late, "hist", QUAD)
    sent = after(sent, back_near)
    kept = kept.reshape(QUAD, n_hist // QUAD, share, wide)
    sent = sent.reshape(n_batch - 1, QUAD, n_hist // QUAD, share, wide)
    total = kept
    for index in range(1, n_batch):
        total = total + swap(sent[index - 1], "batch", index).astype(F32)
    parts = [swap(total[index].astype(BF16), "hist", index) for index in range(1, QUAD)]
    back_late = after(back_late, parts[0])
    level = total[0]
    for part in parts:
        level = level + part.astype(F32)

    def join(index):
        own = [(out_near, dq_near)[index], (out_late, dq_late)[index]]
        back = [back_near[index], back_late[index]]
        return jnp.where(
            side == 0, jnp.concatenate(own + back, axis=1), jnp.concatenate(back + own, axis=1)
        )

    attended = join(0)
    d_targets = lax.dot_general(
        join(1), w_query, (((1,), (1,)), ((), ())), preferred_element_type=F32
    ).astype(BF16)
    level = after(level, (attended, d_targets))

    sums = [level[0], None]
    for index in range(1, n_hist // QUAD):
        got = swap(level[index].astype(BF16), "hist", QUAD * index).astype(F32)
        sums[index % PAIR] = got if sums[index % PAIR] is None else sums[index % PAIR] + got
    d_query_weight = jnp.where(
        side == 0, jnp.concatenate(sums, axis=1), jnp.concatenate(sums[::-1], axis=1)
    )
    return (attended[None], d_targets[None], d_query_weight)


def solution(mesh):
    in_specs = (
        P("batch", "hist", None),
        P(),
        P("batch", "hist", None),
        P("batch", "hist", None),
        P("batch", None, None),
        P("batch"),
        P("batch", "hist", None),
    )
    out_specs = (P("batch", "hist", None), P("batch", "hist", None), P(("hist", "batch"), None))
    return jax.shard_map(shards, mesh=mesh, in_specs=in_specs, out_specs=out_specs, check_vma=False)
```

```python
import functools

import jax
import jax.numpy as jnp
from jax import lax
from jax.experimental import pallas as pl
from jax.experimental.pallas import tpu as pltpu
from jax.sharding import PartitionSpec as P

BLK = 64
LANES = 128
TILE = 16
QUAD = 4
PAIR = 2
DEAD = -1e30
VMEM_LIMIT = 60 * 1024 * 1024
VMEM_SOURCE = 1280 * 1024
CUT = 2
F32 = jnp.float32
BF16 = jnp.bfloat16


def swap(array, axis, mask):
    size = lax.axis_size(axis)
    return lax.ppermute(array, axis, [(i, i ^ mask) for i in range(size)])


def after(array, other):
    return lax.optimization_barrier((array, other))[0]


def select_kernel(cut, blocks_ref, lengths_ref, keys_ref, values_ref, *outs):
    heads, topk = blocks_ref.shape[1:]
    rows, width = keys_ref.shape[1:]
    half = heads // PAIR
    head_dim = width // heads
    blk_dev = rows // BLK
    rank = lax.axis_index("hist")
    side = (rank // QUAD) % PAIR
    length = lengths_ref[0]
    count = half * blk_dev
    room = -(-count // TILE) * TILE
    keep_near, keep_late, send_near, send_all = outs
    near_rows = keep_near.shape[0]
    sides = (
        (side * half, ((keep_near, 0),), ((keep_late, 0),)),
        ((1 - side) * half, ((send_near, 0), (send_all, 0)), ((send_all, near_rows),)),
    )
    for first, near, late in sides:
        for index in range(half):
            head = first + index
            local = jnp.int32(0)
            for entry in range(topk):
                block = blocks_ref[0, head, entry] - rank * blk_dev
                local = jnp.where((block >= 0) & (block < blk_dev), block, local)
            low = pl.multiple_of(local * BLK, BLK)
            at = (index - (cut if index >= cut else 0)) * BLK
            columns = pl.ds(pl.multiple_of(head * head_dim, head_dim), head_dim)
            key = keys_ref[0, pl.ds(low, BLK), columns]
            value = values_ref[0, pl.ds(low, BLK), columns]
            for out, base in late if index >= cut else near:
                out[base + at : base + at + BLK, :head_dim] = key
                out[base + at : base + at + BLK, head_dim:] = value
        span = pl.ds(pl.multiple_of(first * head_dim, head_dim), half * head_dim)
        for source, low in ((keys_ref, 0), (values_ref, head_dim)):
            totals = []
            for block in range(blk_dev):
                part = source[0, block * BLK : (block + 1) * BLK, span].astype(F32)
                spot = lax.broadcasted_iota(jnp.int32, part.shape, 0) + (rank * rows + block * BLK)
                part = jnp.where(spot < length, part, 0.0)
                totals.append(jnp.sum(part, axis=0, keepdims=True) * BLK ** (-0.5))
            lines = [
                totals[block][:, index * head_dim : (index + 1) * head_dim]
                for index in range(half)
                for block in range(blk_dev)
            ]
            lines.append(jnp.zeros((room - count, head_dim), F32))
            summary = jnp.concatenate(lines, axis=0).astype(BF16)
            for out, _ in near:
                out[cut * BLK : cut * BLK + room, low : low + head_dim] = summary


def attend_kernel(pieces, fine_width, scale, *refs):
    bias_ref = refs[0]
    inputs = (refs[1:3], refs[4:6])
    own_order, their_order = refs[3], refs[6]
    piece_refs = refs[7 : 7 + pieces]
    out_ref, dq_ref, away_ref, keep_ref, send_ref = refs[-5:]
    head_dim = out_ref.shape[1]
    keys = jnp.concatenate(
        [r[:, :, :head_dim].reshape(-1, head_dim) for r in piece_refs], axis=0
    )
    values = jnp.concatenate(
        [r[:, :, head_dim:].reshape(-1, head_dim) for r in piece_refs], axis=0
    )
    bias = bias_ref[0]
    cols = (slice(0, fine_width), slice(fine_width, keys.shape[0]))
    contract = (((1,), (1,)), ((), ()))
    query, grad = (jnp.concatenate([own[...], their[...]]) for own, their in zip(*inputs))
    scores = lax.dot_general(query, keys, contract, preferred_element_type=F32) * scale + bias
    d_probs = lax.dot_general(grad, values, contract, preferred_element_type=F32)
    probs_parts = []
    d_parts = []
    for part in cols:
        score = scores[:, part]
        expo = jnp.exp(score - jnp.max(score, axis=1, keepdims=True))
        probs = expo * (1.0 / jnp.sum(expo, axis=1, keepdims=True))
        d_prob = d_probs[:, part]
        delta = jnp.sum(probs * d_prob, axis=1, keepdims=True)
        probs_parts.append(probs.astype(BF16))
        d_parts.append((probs * (d_prob - delta)).astype(BF16))
    out = jnp.dot(jnp.concatenate(probs_parts, axis=1), values, preferred_element_type=F32)
    d_query = jnp.dot(jnp.concatenate(d_parts, axis=1), keys, preferred_element_type=F32)
    out = out.astype(BF16)
    d_query = (d_query * scale).astype(BF16)
    rows = out_ref.shape[0]
    out_ref[...] = out[:rows]
    dq_ref[...] = d_query[:rows]
    away_ref[0] = out[rows:]
    away_ref[1] = d_query[rows:]
    weight = jnp.dot(own_order[...], d_query[:rows], preferred_element_type=F32)
    weight += jnp.dot(their_order[...], d_query[rows:], preferred_element_type=F32)
    kept = keep_ref.shape[0]
    keep_ref[...] = weight[:kept]
    send_ref[...] = weight[kept:].astype(BF16)


def attend(first, count, bias, own_side, their_side, summaries, pieces, share, earlier):
    rows = own_side[0].shape[0]
    depth = own_side[2].shape[0]
    half = bias.shape[0]
    width = own_side[0].shape[1]
    head_dim = width // half
    fine_width = sum(p.shape[0] for p in pieces) * BLK
    room = (bias.shape[-1] - fine_width) // sum(p.shape[0] for p in pieces)
    kept = depth // share
    in_specs = [pl.BlockSpec((1,) + bias.shape[1:], lambda i: (first + i, 0, 0))]
    for at in (0, own_side[1].shape[0] // rows - 1), (0, their_side[1].shape[0] // rows - 1):
        in_specs += [
            pl.BlockSpec((rows, head_dim), lambda i, at=at[0]: (at, first + i)),
            pl.BlockSpec((rows, head_dim), lambda i, at=at[1]: (at, first + i)),
            pl.BlockSpec((depth, rows), lambda i: (0, 0)),
        ]
    in_specs += [
        pl.BlockSpec((p.shape[0], BLK, 2 * head_dim), lambda i: (0, i, 0)) for p in pieces
    ]
    in_specs += [
        pl.BlockSpec((p.shape[0], room, 2 * head_dim), lambda i: (0, CUT * BLK // room, 0))
        for p in summaries
    ]
    args = [bias, *own_side, *their_side, *pieces, *summaries]
    aliases = {}
    if earlier is not None:
        aliases = {len(args) + i: 3 + i for i in range(len(earlier))}
        args += list(earlier)
        in_specs += [pl.BlockSpec(memory_space=pl.ANY)] * len(earlier)
    own = jax.ShapeDtypeStruct((rows, count * head_dim), BF16)
    own_spec = pl.BlockSpec((rows, head_dim), lambda i: (0, i))
    columns = bias.shape[-1]
    return pl.pallas_call(
        functools.partial(attend_kernel, len(pieces) + len(summaries), fine_width, head_dim ** (-0.5)),
        grid=(count,),
        in_specs=in_specs,
        out_specs=(
            own_spec,
            own_spec,
            pl.BlockSpec((2, rows, head_dim), lambda i: (0, 0, i)),
            pl.BlockSpec((kept, head_dim), lambda i: (0, first + i)),
            pl.BlockSpec((depth - kept, head_dim), lambda i: (0, first + i)),
        ),
        out_shape=(
            own,
            own,
            jax.ShapeDtypeStruct((2,) + own.shape, BF16),
            jax.ShapeDtypeStruct((kept, width), F32),
            jax.ShapeDtypeStruct((depth - kept, width), BF16),
        ),
        input_output_aliases=aliases,
        compiler_params=pltpu.CompilerParams(
            vmem_limit_bytes=min(VMEM_LIMIT, sum(p.shape[0] for p in pieces) * VMEM_SOURCE)
        ),
        cost_estimate=pl.CostEstimate(
            flops=16 * count * rows * columns * head_dim,
            bytes_accessed=count * (columns * 512 + rows * head_dim * 8),
            transcendentals=2 * count * rows * columns,
        ),
        name="attend",
    )(*args)


def gather_quad(column):
    return [column] + [swap(column, "hist", mask) for mask in range(1, QUAD)]


def shards(targets, w_query, keys, values, blocks, lengths, d_attended):
    heads = blocks.shape[1]
    local_rows, width = keys.shape[1:]
    head_dim = width // heads
    blk_dev = local_rows // BLK
    n_hist = lax.axis_size("hist")
    n_batch = lax.axis_size("batch")
    rank = lax.axis_index("hist")
    lane = lax.axis_index("batch")
    rows = targets.shape[1]
    depth = targets.shape[2]
    half = heads // PAIR
    side = (rank // QUAD) % PAIR
    wide = half * head_dim
    count = half * blk_dev
    room = -(-count // TILE) * TILE
    near_rows = CUT * BLK + room
    late_rows = (half - CUT) * BLK
    keep_near, keep_late, send_near, send = pl.pallas_call(
        functools.partial(select_kernel, CUT),
        in_specs=[
            pl.BlockSpec(memory_space=pltpu.SMEM),
            pl.BlockSpec(memory_space=pltpu.SMEM),
            pl.BlockSpec(memory_space=pltpu.VMEM),
            pl.BlockSpec(memory_space=pltpu.VMEM),
        ],
        out_specs=[pl.BlockSpec(memory_space=pltpu.VMEM)] * 4,
        out_shape=[
            jax.ShapeDtypeStruct((size, 2 * head_dim), BF16)
            for size in (near_rows, late_rows, near_rows, near_rows + late_rows)
        ],
        name="select",
    )(blocks, lengths, keys, values)
    came = swap(send, "hist", QUAD)
    column_near = jnp.stack(
        [keep_near, came[:near_rows]]
        + [
            swap((keep_near, send_near)[k % PAIR], "hist", QUAD * k)
            for k in range(PAIR, n_hist // QUAD)
        ]
    )
    near = gather_quad(column_near)
    pair_late = after(jnp.stack([keep_late, came[near_rows:]]), column_near)
    column_late = jnp.concatenate(
        [pair_late]
        + [swap(pair_late, "hist", QUAD * k) for k in range(PAIR, n_hist // QUAD, PAIR)]
    )

    grad = d_attended[0]
    grad_keep = lax.dynamic_slice_in_dim(grad, side * wide, wide, 1)
    grad_send = lax.dynamic_slice_in_dim(grad, (1 - side) * wide, wide, 1)
    theirs = swap(jnp.concatenate([targets[0], grad_send]), "hist", QUAD)
    weights = lax.dynamic_slice_in_dim(w_query, side * wide, wide, 1)

    def project(part):
        return jnp.dot(part, weights, preferred_element_type=F32).astype(BF16)

    masks = jnp.asarray([q + QUAD * k for q in range(QUAD) for k in range(n_hist // QUAD)], jnp.int32)
    source = rank ^ masks
    lists = lax.dynamic_slice_in_dim(blocks[0], side * half, half, 0)
    listed = jnp.max(
        jnp.where((lists // blk_dev)[:, :, None] == source[None, None, :], lists[:, :, None], -1),
        axis=1,
    )
    spots = jnp.arange(BLK, dtype=jnp.int32)
    live = (listed[:, :, None] >= 0) & (listed[:, :, None] * BLK + spots < lengths[0])
    fine_bias = jnp.where(live, 0.0, DEAD).astype(F32).reshape(half, -1)
    line = jnp.arange(room, dtype=jnp.int32)
    names = source[:, None] * blk_dev + line[None, :] % blk_dev
    own_line = (line // blk_dev)[None, :] == jnp.arange(half, dtype=jnp.int32)[:, None]
    coarse_live = own_line[:, None, :] & (names * BLK < lengths[0])[None]
    coarse_bias = jnp.where(coarse_live, 0.0, DEAD).astype(F32).reshape(half, -1)
    fine_bias = after(fine_bias, column_near)
    bias = jnp.concatenate([fine_bias, coarse_bias], axis=1)[:, None, :]

    places = (
        (rank ^ masks)[None, :] * n_batch + (lane ^ jnp.arange(n_batch, dtype=jnp.int32))[:, None]
    ).reshape(-1)
    share = depth // (n_hist * n_batch)
    chosen = (places[:, None] * share + jnp.arange(share, dtype=jnp.int32)).reshape(-1)
    shuffle = (chosen[:, None] == jnp.arange(depth, dtype=jnp.int32)[None, :]).astype(BF16)

    def reorder(part):
        product = lax.dot_general(
            shuffle, part, (((1,), (1,)), ((), ())), preferred_element_type=F32
        )
        return product.astype(BF16)

    own_side = (project(targets[0]), grad_keep, reorder(targets[0]))
    their_side = (project(theirs[:rows]), theirs, reorder(theirs[:rows]))
    late = gather_quad(after(column_late, theirs))
    fixed = (bias, own_side, their_side, near)
    out_near, dq_near, away_near, *weight = attend(0, CUT, *fixed, near, n_batch, None)
    out_late, dq_late, away_late, kept, sent = attend(
        CUT, half - CUT, *fixed, late, n_batch, weight
    )

    back_near = swap(away_near, "hist", QUAD)
    back_late = swap(away_late, "hist", QUAD)
    sent = after(sent, back_near)
    kept = kept.reshape(QUAD, n_hist // QUAD, share, wide)
    sent = sent.reshape(n_batch - 1, QUAD, n_hist // QUAD, share, wide)
    total = kept
    for index in range(1, n_batch):
        total = total + swap(sent[index - 1], "batch", index).astype(F32)
    parts = [swap(total[index].astype(BF16), "hist", index) for index in range(1, QUAD)]
    back_late = after(back_late, parts[0])
    level = total[0]
    for part in parts:
        level = level + part.astype(F32)

    taken = [swap(level[k].astype(BF16), "hist", QUAD * k) for k in range(1, n_hist // QUAD)]
    sums = [level[0], None]
    for index, part in enumerate(taken, 1):
        got = part.astype(F32)
        sums[index % PAIR] = got if sums[index % PAIR] is None else sums[index % PAIR] + got

    def join(index):
        own = [(out_near, dq_near)[index], (out_late, dq_late)[index]]
        back = [back_near[index], back_late[index]]
        return jnp.where(
            side == 0, jnp.concatenate(own + back, axis=1), jnp.concatenate(back + own, axis=1)
        )

    attended = join(0)
    d_targets = lax.dot_general(
        join(1), w_query, (((1,), (1,)), ((), ())), preferred_element_type=F32
    ).astype(BF16)

    d_query_weight = jnp.where(
        side == 0, jnp.concatenate(sums, axis=1), jnp.concatenate(sums[::-1], axis=1)
    )
    return (attended[None], d_targets[None], d_query_weight)


def solution(mesh):
    in_specs = (
        P("batch", "hist", None),
        P(),
        P("batch", "hist", None),
        P("batch", "hist", None),
        P("batch", None, None),
        P("batch"),
        P("batch", "hist", None),
    )
    out_specs = (P("batch", "hist", None), P("batch", "hist", None), P(("hist", "batch"), None))
    return jax.shard_map(shards, mesh=mesh, in_specs=in_specs, out_specs=out_specs, check_vma=False)
```

```python
import functools

import jax
import jax.numpy as jnp
from jax import lax
from jax.experimental import pallas as pl
from jax.experimental.pallas import tpu as pltpu
from jax.sharding import PartitionSpec as P

BLK = 64
LANES = 128
TILE = 16
QUAD = 4
PAIR = 2
DEAD = -1e30
VMEM_LIMIT = 60 * 1024 * 1024
VMEM_SOURCE = 1280 * 1024
CUT = 2
F32 = jnp.float32
BF16 = jnp.bfloat16


def swap(array, axis, mask):
    size = lax.axis_size(axis)
    return lax.ppermute(array, axis, [(i, i ^ mask) for i in range(size)])


def after(array, other):
    return lax.optimization_barrier((array, other))[0]


def select_kernel(cut, blocks_ref, lengths_ref, keys_ref, values_ref, *outs):
    heads, topk = blocks_ref.shape[1:]
    rows, width = keys_ref.shape[1:]
    half = heads // PAIR
    head_dim = width // heads
    blk_dev = rows // BLK
    rank = lax.axis_index("hist")
    side = (rank // QUAD) % PAIR
    length = lengths_ref[0]
    count = half * blk_dev
    room = -(-count // TILE) * TILE
    keep_near, keep_late, send_near, send_all = outs
    near_rows = keep_near.shape[0]
    sides = (
        (side * half, ((keep_near, 0),), ((keep_late, 0),)),
        ((1 - side) * half, ((send_near, 0), (send_all, 0)), ((send_all, near_rows),)),
    )
    for first, near, late in sides:
        for index in range(half):
            head = first + index
            local = jnp.int32(0)
            for entry in range(topk):
                block = blocks_ref[0, head, entry] - rank * blk_dev
                local = jnp.where((block >= 0) & (block < blk_dev), block, local)
            low = pl.multiple_of(local * BLK, BLK)
            at = (index - (cut if index >= cut else 0)) * BLK
            columns = pl.ds(pl.multiple_of(head * head_dim, head_dim), head_dim)
            key = keys_ref[0, pl.ds(low, BLK), columns]
            value = values_ref[0, pl.ds(low, BLK), columns]
            for out, base in late if index >= cut else near:
                out[base + at : base + at + BLK, :head_dim] = key
                out[base + at : base + at + BLK, head_dim:] = value
        span = pl.ds(pl.multiple_of(first * head_dim, head_dim), half * head_dim)
        for source, low in ((keys_ref, 0), (values_ref, head_dim)):
            totals = []
            for block in range(blk_dev):
                part = source[0, block * BLK : (block + 1) * BLK, span].astype(F32)
                spot = lax.broadcasted_iota(jnp.int32, part.shape, 0) + (rank * rows + block * BLK)
                part = jnp.where(spot < length, part, 0.0)
                totals.append(jnp.sum(part, axis=0, keepdims=True) * BLK ** (-0.5))
            lines = [
                totals[block][:, index * head_dim : (index + 1) * head_dim]
                for index in range(half)
                for block in range(blk_dev)
            ]
            lines.append(jnp.zeros((room - count, head_dim), F32))
            summary = jnp.concatenate(lines, axis=0).astype(BF16)
            for out, _ in near:
                out[cut * BLK : cut * BLK + room, low : low + head_dim] = summary


def attend_kernel(pieces, fine_width, scale, *refs):
    bias_ref = refs[0]
    inputs = (refs[1:3], refs[4:6])
    own_order, their_order = refs[3], refs[6]
    piece_refs = refs[7 : 7 + pieces]
    out_ref, dq_ref, away_ref, keep_ref, send_ref = refs[-5:]
    head_dim = out_ref.shape[1]
    keys = jnp.concatenate(
        [r[..., :head_dim].reshape(-1, head_dim) for r in piece_refs], axis=0
    )
    values = jnp.concatenate(
        [r[..., head_dim:].reshape(-1, head_dim) for r in piece_refs], axis=0
    )
    bias = bias_ref[0]
    cols = (slice(0, fine_width), slice(fine_width, keys.shape[0]))
    contract = (((1,), (1,)), ((), ()))
    query, grad = (jnp.concatenate([own[...], their[...]]) for own, their in zip(*inputs))
    scores = lax.dot_general(query, keys, contract, preferred_element_type=F32) * scale + bias
    d_probs = lax.dot_general(grad, values, contract, preferred_element_type=F32)
    probs_parts = []
    d_parts = []
    for part in cols:
        score = scores[:, part]
        expo = jnp.exp(score - jnp.max(score, axis=1, keepdims=True))
        probs = expo * (1.0 / jnp.sum(expo, axis=1, keepdims=True))
        d_prob = d_probs[:, part]
        delta = jnp.sum(probs * d_prob, axis=1, keepdims=True)
        probs_parts.append(probs.astype(BF16))
        d_parts.append((probs * (d_prob - delta)).astype(BF16))
    out = jnp.dot(jnp.concatenate(probs_parts, axis=1), values, preferred_element_type=F32)
    d_query = jnp.dot(jnp.concatenate(d_parts, axis=1), keys, preferred_element_type=F32)
    out = out.astype(BF16)
    d_query = (d_query * scale).astype(BF16)
    rows = out_ref.shape[0]
    out_ref[...] = out[:rows]
    dq_ref[...] = d_query[:rows]
    away_ref[0] = out[rows:]
    away_ref[1] = d_query[rows:]
    weight = jnp.dot(own_order[...], d_query[:rows], preferred_element_type=F32)
    weight += jnp.dot(their_order[...], d_query[rows:], preferred_element_type=F32)
    kept = keep_ref.shape[0]
    keep_ref[...] = weight[:kept]
    send_ref[...] = weight[kept:].astype(BF16)


def attend(first, count, bias, own_side, their_side, summaries, pieces, share, earlier):
    rows = own_side[0].shape[0]
    depth = own_side[2].shape[0]
    half = bias.shape[0]
    width = own_side[0].shape[1]
    head_dim = width // half
    sources = lax.axis_size("hist")
    fine_width = sources * BLK
    room = bias.shape[-1] // sources - BLK
    kept = depth // share
    in_specs = [pl.BlockSpec((1,) + bias.shape[1:], lambda i: (first + i, 0, 0))]
    for at in (0, own_side[1].shape[0] // rows - 1), (0, their_side[1].shape[0] // rows - 1):
        in_specs += [
            pl.BlockSpec((rows, head_dim), lambda i, at=at[0]: (at, first + i)),
            pl.BlockSpec((rows, head_dim), lambda i, at=at[1]: (at, first + i)),
            pl.BlockSpec((depth, rows), lambda i: (0, 0)),
        ]
    rest = sources // QUAD
    in_specs += [
        pl.BlockSpec((rest * BLK, 2 * head_dim), lambda i: (i, 0))
        if p.ndim == 2
        else pl.BlockSpec((rest, BLK, 2 * head_dim), lambda i: (0, i, 0))
        for p in pieces
    ]
    in_specs += [
        pl.BlockSpec((rest * room, 2 * head_dim), lambda i: (CUT * BLK // room, 0))
        for _ in summaries
    ]
    args = [bias, *own_side, *their_side, *pieces, *summaries]
    aliases = {}
    if earlier is not None:
        aliases = {len(args) + i: 3 + i for i in range(len(earlier))}
        args += list(earlier)
        in_specs += [pl.BlockSpec(memory_space=pl.ANY)] * len(earlier)
    own = jax.ShapeDtypeStruct((rows, count * head_dim), BF16)
    own_spec = pl.BlockSpec((rows, head_dim), lambda i: (0, i))
    columns = bias.shape[-1]
    return pl.pallas_call(
        functools.partial(attend_kernel, len(pieces) + len(summaries), fine_width, head_dim ** (-0.5)),
        grid=(count,),
        in_specs=in_specs,
        out_specs=(
            own_spec,
            own_spec,
            pl.BlockSpec((2, rows, head_dim), lambda i: (0, 0, i)),
            pl.BlockSpec((kept, head_dim), lambda i: (0, first + i)),
            pl.BlockSpec((depth - kept, head_dim), lambda i: (0, first + i)),
        ),
        out_shape=(
            own,
            own,
            jax.ShapeDtypeStruct((2,) + own.shape, BF16),
            jax.ShapeDtypeStruct((kept, width), F32),
            jax.ShapeDtypeStruct((depth - kept, width), BF16),
        ),
        input_output_aliases=aliases,
        compiler_params=pltpu.CompilerParams(
            vmem_limit_bytes=min(VMEM_LIMIT, sources * VMEM_SOURCE)
        ),
        cost_estimate=pl.CostEstimate(
            flops=16 * count * rows * columns * head_dim,
            bytes_accessed=count * (columns * 512 + rows * head_dim * 8),
            transcendentals=2 * count * rows * columns,
        ),
        name="attend",
    )(*args)


def gather_quad(column):
    return [column] + [swap(column, "hist", mask) for mask in range(1, QUAD)]


def shards(targets, w_query, keys, values, blocks, lengths, d_attended):
    heads = blocks.shape[1]
    local_rows, width = keys.shape[1:]
    head_dim = width // heads
    blk_dev = local_rows // BLK
    n_hist = lax.axis_size("hist")
    n_batch = lax.axis_size("batch")
    rank = lax.axis_index("hist")
    lane = lax.axis_index("batch")
    rows = targets.shape[1]
    depth = targets.shape[2]
    half = heads // PAIR
    side = (rank // QUAD) % PAIR
    wide = half * head_dim
    count = half * blk_dev
    room = -(-count // TILE) * TILE
    near_rows = CUT * BLK + room
    late_rows = (half - CUT) * BLK
    keep_near, keep_late, send_near, send = pl.pallas_call(
        functools.partial(select_kernel, CUT),
        in_specs=[
            pl.BlockSpec(memory_space=pltpu.SMEM),
            pl.BlockSpec(memory_space=pltpu.SMEM),
            pl.BlockSpec(memory_space=pltpu.VMEM),
            pl.BlockSpec(memory_space=pltpu.VMEM),
        ],
        out_specs=[pl.BlockSpec(memory_space=pltpu.VMEM)] * 4,
        out_shape=[
            jax.ShapeDtypeStruct((size, 2 * head_dim), BF16)
            for size in (near_rows, late_rows, near_rows, near_rows + late_rows)
        ],
        name="select",
    )(blocks, lengths, keys, values)
    came = swap(send, "hist", QUAD)
    column_near = jnp.stack(
        [keep_near, came[:near_rows]]
        + [
            swap((keep_near, send_near)[k % PAIR], "hist", QUAD * k)
            for k in range(PAIR, n_hist // QUAD)
        ]
    )
    packed = column_near[:, : CUT * BLK].reshape(-1, CUT, BLK, 2 * head_dim)
    packed = packed.transpose(1, 0, 2, 3).reshape(-1, 2 * head_dim)
    lines = column_near[:, CUT * BLK : CUT * BLK + count].reshape(-1, 2 * head_dim)
    near = gather_quad(jnp.concatenate([packed, lines]))
    pair_late = after(jnp.stack([keep_late, came[near_rows:]]), column_near)
    column_late = jnp.concatenate(
        [pair_late]
        + [swap(pair_late, "hist", QUAD * k) for k in range(PAIR, n_hist // QUAD, PAIR)]
    )

    grad = d_attended[0]
    grad_keep = lax.dynamic_slice_in_dim(grad, side * wide, wide, 1)
    grad_send = lax.dynamic_slice_in_dim(grad, (1 - side) * wide, wide, 1)
    theirs = swap(jnp.concatenate([targets[0], grad_send]), "hist", QUAD)
    weights = lax.dynamic_slice_in_dim(w_query, side * wide, wide, 1)

    def project(part):
        return jnp.dot(part, weights, preferred_element_type=F32).astype(BF16)

    masks = jnp.asarray([q + QUAD * k for q in range(QUAD) for k in range(n_hist // QUAD)], jnp.int32)
    source = rank ^ masks
    lists = lax.dynamic_slice_in_dim(blocks[0], side * half, half, 0)
    listed = jnp.max(
        jnp.where((lists // blk_dev)[:, :, None] == source[None, None, :], lists[:, :, None], -1),
        axis=1,
    )
    spots = jnp.arange(BLK, dtype=jnp.int32)
    live = (listed[:, :, None] >= 0) & (listed[:, :, None] * BLK + spots < lengths[0])
    fine_bias = jnp.where(live, 0.0, DEAD).astype(F32).reshape(half, -1)
    line = jnp.arange(count, dtype=jnp.int32)
    names = source[:, None] * blk_dev + line[None, :] % blk_dev
    own_line = (line // blk_dev)[None, :] == jnp.arange(half, dtype=jnp.int32)[:, None]
    coarse_live = own_line[:, None, :] & (names * BLK < lengths[0])[None]
    coarse_bias = jnp.where(coarse_live, 0.0, DEAD).astype(F32).reshape(half, -1)
    fine_bias = after(fine_bias, column_near)
    bias = jnp.concatenate([fine_bias, coarse_bias], axis=1)[:, None, :]

    places = (
        (rank ^ masks)[None, :] * n_batch + (lane ^ jnp.arange(n_batch, dtype=jnp.int32))[:, None]
    ).reshape(-1)
    share = depth // (n_hist * n_batch)
    chosen = (places[:, None] * share + jnp.arange(share, dtype=jnp.int32)).reshape(-1)
    shuffle = (chosen[:, None] == jnp.arange(depth, dtype=jnp.int32)[None, :]).astype(BF16)

    def reorder(part):
        product = lax.dot_general(
            shuffle, part, (((1,), (1,)), ((), ())), preferred_element_type=F32
        )
        return product.astype(BF16)

    own_side = (project(targets[0]), grad_keep, reorder(targets[0]))
    their_side = (project(theirs[:rows]), theirs, reorder(theirs[:rows]))
    late = gather_quad(column_late)
    fixed = (bias, own_side, their_side, near)
    out_near, dq_near, away_near, *weight = attend(0, CUT, *fixed, near, n_batch, None)
    out_late, dq_late, away_late, kept, sent = attend(
        CUT, half - CUT, *fixed, late, n_batch, weight
    )

    back_near = swap(away_near, "hist", QUAD)
    back_late = swap(away_late, "hist", QUAD)
    kept = after(kept, back_near)
    kept = kept.reshape(QUAD, n_hist // QUAD, share, wide)
    sent = sent.reshape(n_batch - 1, QUAD, n_hist // QUAD, share, wide)
    total = kept
    for index in range(1, n_batch):
        total = total + swap(sent[index - 1], "batch", index).astype(F32)
    parts = [swap(total[index].astype(BF16), "hist", index) for index in range(1, QUAD)]
    back_late = after(back_late, parts[0])
    level = total[0]
    for part in parts:
        level = level + part.astype(F32)

    taken = [swap(level[k].astype(BF16), "hist", QUAD * k) for k in range(1, n_hist // QUAD)]
    sums = [level[0], None]
    for index, part in enumerate(taken, 1):
        got = part.astype(F32)
        sums[index % PAIR] = got if sums[index % PAIR] is None else sums[index % PAIR] + got

    def join(index):
        own = [(out_near, dq_near)[index], (out_late, dq_late)[index]]
        back = [back_near[index], back_late[index]]
        return jnp.where(
            side == 0, jnp.concatenate(own + back, axis=1), jnp.concatenate(back + own, axis=1)
        )

    attended = join(0)
    d_targets = lax.dot_general(
        join(1), w_query, (((1,), (1,)), ((), ())), preferred_element_type=F32
    ).astype(BF16)

    d_query_weight = jnp.where(
        side == 0, jnp.concatenate(sums, axis=1), jnp.concatenate(sums[::-1], axis=1)
    )
    return (attended[None], d_targets[None], d_query_weight)


def solution(mesh):
    in_specs = (
        P("batch", "hist", None),
        P(),
        P("batch", "hist", None),
        P("batch", "hist", None),
        P("batch", None, None),
        P("batch"),
        P("batch", "hist", None),
    )
    out_specs = (P("batch", "hist", None), P("batch", "hist", None), P(("hist", "batch"), None))
    return jax.shard_map(shards, mesh=mesh, in_specs=in_specs, out_specs=out_specs, check_vma=False)
```
